32 devices in a mesh: groups: 2 (over x), tm: 4 (over y, core), chan: 4 (over z).
Axes of the slice: x: 2, y: 2, z: 4, core: 2. Of those that a mesh axis runs over, the one named last changes fastest.
Arguments:
- records: bfloat16 [1536, 1024], P(('groups', 'tm'), 'chan'), parts along dimension 0, may hold values from -6 to 6
- cotangent: bfloat16 [1536, 1024], P(('groups', 'tm'), 'chan'), parts along dimension 0, may hold values from -6 to 6
- filter_weight: bfloat16 [4, 2, 1024, 1024], P(None, None, 'tm', 'chan'), may hold values from -0.125 to 0.125
- gate_weight: bfloat16 [4, 2, 1024, 1024], P(None, None, 'tm', 'chan'), may hold values from -0.125 to 0.125
- mix_weight: bfloat16 [4, 1024, 1024], P(None, 'chan', 'tm'), may hold values from -0.1875 to 0.1875
Outputs:
- output: bfloat16 [1536, 1024], P(('groups', 'tm'), 'chan'), parts along dimension 0
- input_grad: bfloat16 [1536, 1024], P(('groups', 'tm'), 'chan'), parts along dimension 0
The draws below stay inside these ranges and needn't reach their ends.
There are 2 independent parts, one for each index of `groups`. The reference program is written for one: setup_inputs(seed, part) draws one part's arguments, and reference() takes and returns one part's arrays. A program takes and returns all parts, laid end to end along the dimension named above; an argument that names none is the same for every part. Nothing has to cross between parts.
All inputs are finite; a program needn't handle non-finite values.
Results may differ from the reference program's by a relative error of at most 0.018.
Values may be sent and summed in bfloat16 or wider, within the bound.
No kernel may reach another device: no remote copies, remote signals or barrier semaphores. Data moves between devices by JAX's collectives and lax.ppermute only.
A program may use at most 64 MiB of HBM per device.

```python
import jax
import jax.numpy as jnp

C = 1024
LAYERS = 4
T_DEV = 192
TIME = 768


def block_levels(stream_key, dims, cuts, least, largest):
    factor_of, own = 1.0, jax.random.fold_in(stream_key, 6)
    for dim, parts in cuts:
        steps = jnp.exp(jax.random.uniform(jax.random.fold_in(own, dim), (parts,), jnp.float32, least / len(cuts), largest / len(cuts)))
        factor_of = factor_of * jnp.repeat(steps, dims[dim] // parts).reshape([-1 if axis == dim else 1 for axis in range(len(dims))])
    return factor_of


def noise(rng, shape, spread, reach, shards=(), held_as=jnp.bfloat16):
    factor_of = block_levels(rng, shape, shards, -0.22, 0.18) if shards else 1.0
    drawn = jax.random.normal(rng, shape, jnp.float32) * spread * factor_of
    return jnp.minimum(jnp.maximum(drawn, -reach), reach).astype(held_as)


def setup_inputs(seed: int = 0, part: int = 0) -> dict:
    splits = jax.random.split(jax.random.key(seed), 6)
    own_keys = jax.random.split(jax.random.fold_in(splits[5], part), 6)
    records = noise(own_keys[0], (TIME, C), 1.0, 6.0, ((0, 4), (1, 4)))
    cotangent = noise(own_keys[1], (TIME, C), 1.0, 6.0, ((0, 4), (1, 4)))
    filter_weight = noise(splits[2], (LAYERS, 2, C, C), (2 * C) ** -0.5, 0.125, ((2, 4), (3, 4)))
    gate_weight = noise(splits[3], (LAYERS, 2, C, C), (2 * C) ** -0.5, 0.125, ((2, 4), (3, 4)))
    mix_weight = noise(splits[4], (LAYERS, C, C), C ** -0.5, 0.1875, ((1, 4), (2, 4)))
    return {"records": records, "cotangent": cotangent, "filter_weight": filter_weight, "gate_weight": gate_weight, "mix_weight": mix_weight}


def delay_rows(values, span):
    count = values.shape[0]
    if span >= count:
        return jnp.zeros_like(values)
    head = jnp.zeros((span, values.shape[1]), values.dtype)
    return jnp.concatenate([head, values[:count - span]], axis=0)


def advance_rows(values, span):
    count = values.shape[0]
    if span >= count:
        return jnp.zeros_like(values)
    tail = jnp.zeros((span, values.shape[1]), values.dtype)
    return jnp.concatenate([values[span:], tail], axis=0)


def reference(records, cotangent, filter_weight, gate_weight, mix_weight):
    signal = records
    stored = []
    for layer_index in range(LAYERS):
        span_rows = T_DEV * 2 ** layer_index
        delayed = delay_rows(signal, span_rows)
        pre_filter = jnp.dot(delayed, filter_weight[layer_index, 0], preferred_element_type=jnp.float32) + jnp.dot(signal, filter_weight[layer_index, 1], preferred_element_type=jnp.float32)
        pre_gate = jnp.dot(delayed, gate_weight[layer_index, 0], preferred_element_type=jnp.float32) + jnp.dot(signal, gate_weight[layer_index, 1], preferred_element_type=jnp.float32)
        gated = (jnp.tanh(pre_filter) * jax.nn.sigmoid(pre_gate)).astype(jnp.bfloat16)
        mix_term = jnp.dot(gated, mix_weight[layer_index], preferred_element_type=jnp.float32)
        signal = (signal.astype(jnp.float32) + mix_term).astype(jnp.bfloat16)
        stored.append((pre_filter, pre_gate))
    output = signal
    grad_now = cotangent
    for layer_index in reversed(range(LAYERS)):
        span_rows = T_DEV * 2 ** layer_index
        pre_filter, pre_gate = stored[layer_index]
        grad_z = jnp.dot(grad_now, mix_weight[layer_index].T, preferred_element_type=jnp.float32)
        tanh_value = jnp.tanh(pre_filter)
        sig_value = jax.nn.sigmoid(pre_gate)
        grad_filt = (grad_z * sig_value * (1.0 - tanh_value * tanh_value)).astype(jnp.bfloat16)
        grad_gate = (grad_z * tanh_value * sig_value * (1.0 - sig_value)).astype(jnp.bfloat16)
        near_term = jnp.dot(grad_filt, filter_weight[layer_index, 1].T, preferred_element_type=jnp.float32) + jnp.dot(grad_gate, gate_weight[layer_index, 1].T, preferred_element_type=jnp.float32)
        far_term = jnp.dot(grad_filt, filter_weight[layer_index, 0].T, preferred_element_type=jnp.float32) + jnp.dot(grad_gate, gate_weight[layer_index, 0].T, preferred_element_type=jnp.float32)
        grad_now = (grad_now.astype(jnp.float32) + near_term + advance_rows(far_term, span_rows)).astype(jnp.bfloat16)
    return output, grad_now
```

```python
import functools

import jax
import jax.numpy as jnp
from jax import lax
from jax.experimental import pallas as pl
from jax.experimental.pallas import tpu as pltpu
from jax.sharding import PartitionSpec as P

BOTH = ("tm", "chan")


def dot(left, right):
    return jnp.dot(left, right, preferred_element_type=jnp.float32)


def dot_t(left, right):
    return lax.dot_general(
        left, right, (((1,), (1,)), ((), ())), preferred_element_type=jnp.float32
    )


class Blocks:
    def __init__(self, refs, kblocks, jblocks, taps, kb, half):
        self.refs, self.jblocks, self.taps, self.kb, self.half = refs, jblocks, taps, kb, half
        self.kblocks = kblocks

    def tap(self, which, i, j):
        return self.refs[0][i * self.jblocks + j, pl.ds(which * self.kb, self.kb), :]

    def mix(self, i, j):
        if len(self.refs) == 1:
            return self.refs[0][i * self.jblocks + j, pl.ds(self.taps * self.kb, self.half), :]
        return self.refs[1][i * self.jblocks + j]


def down(values, rows):
    return jnp.concatenate([jnp.zeros_like(values[:rows]), values[: values.shape[0] - rows]], axis=0)


def up(values, rows):
    return jnp.concatenate([values[rows:], jnp.zeros_like(values[:rows])], axis=0)


def total(parts):
    if len(parts) == 1:
        return parts[0][...]
    base, own, other = (part[...].astype(jnp.float32) for part in parts)
    return (base + (own + other)).astype(jnp.bfloat16)


def forward_part(blocks, x_ref, shift, fac_f, fac_g, part_ref, acc_ref):
    kb, half = blocks.kb, blocks.half
    current = blocks.taps - 1
    for j in range(blocks.jblocks):
        near = far = None
        for i in range(blocks.kblocks):
            x = x_ref[:, pl.ds(i * kb, kb)]
            term = dot(x, blocks.tap(current, i, j))
            near = term if near is None else near + term
            if blocks.taps == 2:
                term = dot(x, blocks.tap(0, i, j))
                far = term if far is None else far + term
        pre = near if far is None else near + down(far, shift)
        tanh_value = jnp.tanh(pre[:, :half])
        sig_value = jax.nn.sigmoid(pre[:, half:])
        gated = (tanh_value * sig_value).astype(jnp.bfloat16)
        fac_f[j] = sig_value * (1.0 - tanh_value * tanh_value)
        fac_g[j] = tanh_value * sig_value * (1.0 - sig_value)
        for i in range(blocks.kblocks):
            term = dot(gated, blocks.mix(i, j))
            cols = pl.ds(i * kb, kb)
            if j == 0:
                acc_ref[:, cols] = term
            else:
                acc_ref[:, cols] += term
    part_ref[...] = acc_ref[...].astype(jnp.bfloat16)


def backward_part(blocks, g_ref, shift, fac_f, fac_g, part_ref, acc_ref):
    kb = blocks.kb
    current = blocks.taps - 1
    for j in range(blocks.jblocks):
        grad_z = None
        for i in range(blocks.kblocks):
            term = dot_t(g_ref[:, pl.ds(i * kb, kb)], blocks.mix(i, j))
            grad_z = term if grad_z is None else grad_z + term
        both = jnp.concatenate([grad_z * fac_f[j], grad_z * fac_g[j]], axis=1).astype(jnp.bfloat16)
        for i in range(blocks.kblocks):
            term = dot_t(both, blocks.tap(current, i, j))
            if blocks.taps == 2:
                term = term + up(dot_t(both, blocks.tap(0, i, j)), shift)
            cols = pl.ds(i * kb, kb)
            if j == 0:
                acc_ref[:, cols] = term
            else:
                acc_ref[:, cols] += term
    part_ref[...] = acc_ref[...].astype(jnp.bfloat16)


def layer_cost(rows, weights, passes):
    return pl.CostEstimate(
        flops=2 * rows * weights * passes, bytes_accessed=2 * weights, transcendentals=rows * 1024
    )


def call(body, ins, outs, scratch, rows, weights, passes, name):
    vmem = pl.BlockSpec(memory_space=pltpu.VMEM)
    return pl.pallas_call(
        body,
        out_shape=outs,
        in_specs=[vmem] * len(ins),
        out_specs=[vmem] * len(outs),
        scratch_shapes=scratch,
        compiler_params=pltpu.CompilerParams(vmem_limit_bytes=24 * 1024 * 1024),
        cost_estimate=layer_cost(rows, weights, passes),
        name=name,
    )(*ins)


def local(records, cotangent, filter_weight, gate_weight, mix_weight):
    layers = filter_weight.shape[0]
    rows, nb = records.shape
    kb = filter_weight.shape[2]
    tm_count, chan_count = lax.axis_size("tm"), lax.axis_size("chan")
    group = lax.axis_index("groups")
    peers = tm_count * chan_count
    width = nb * chan_count
    half = nb // 2
    bf16, f32 = jnp.bfloat16, jnp.float32

    take = -(-rows // (4 * peers)) * 4
    padded = take * peers

    gathered = []
    for layer in range(layers):
        taps = 2 if 2**layer < tm_count else 1
        halves = [
            lax.dynamic_slice_in_dim(weight[layer, 2 - taps :], group * half, half, 2)
            for weight in (filter_weight, gate_weight)
        ]
        pack = jnp.concatenate(halves, axis=2).reshape(taps * kb, nb)
        mix = lax.dynamic_slice_in_dim(mix_weight[layer], group * half, half, 0)
        packs = [jnp.concatenate([pack, mix], axis=0)] if kb == nb else [pack, mix]
        gathered.append((taps, [lax.all_gather(p, BOTH, axis=0, tiled=False) for p in packs]))

    def swap(values):
        return lax.ppermute(values, "groups", [(0, 1), (1, 0)])

    both = jnp.pad(jnp.stack([records, cotangent]), ((0, 0), (0, padded - rows), (0, 0)))
    sent = both.reshape(2, peers, take, nb).transpose(1, 0, 2, 3)
    got = lax.all_to_all(sent, BOTH, split_axis=0, concat_axis=0, tiled=True)
    got = got.reshape(tm_count, chan_count, 2, take, nb).transpose(2, 0, 3, 1, 4)
    own = got.reshape(2, tm_count, take, width)
    other = swap(own)
    first, second = jnp.where(group == 0, own, other), jnp.where(group == 0, other, own)
    pair = jnp.concatenate([first, second], axis=2)
    m = tm_count * 2 * take
    signal, grad = pair.reshape(2, m, width)

    act = jax.ShapeDtypeStruct((m, width), bf16)
    fac = jax.ShapeDtypeStruct((chan_count, m, half), f32)
    scratch = [pltpu.VMEM((m, width), f32)]

    def shift_of(layer):
        return 2**layer * 2 * take

    def make_blocks(refs, taps):
        return Blocks(refs, tm_count, chan_count, taps, kb, half)

    factors = []
    parts = [signal]
    for layer in range(layers - 1):
        taps, weights = gathered[layer]

        def body(*refs, taps=taps, shift=shift_of(layer), nparts=len(parts), nw=len(weights)):
            ins, (sig, part, fac_f, fac_g, acc) = refs[: nparts + nw], refs[nparts + nw :]
            sig[...] = total(ins[:nparts])
            forward_part(make_blocks(ins[nparts:], taps), sig, shift, fac_f, fac_g, part, acc)

        elems = sum(w.size for w in weights)
        sig, part, fac_f, fac_g = call(
            body, [*parts, *weights], [act, act, fac, fac], scratch, m, elems, 1, "layer_forward"
        )
        factors.append((fac_f, fac_g))
        parts = [sig, part, swap(part)]

    taps, weights = gathered[-1]

    def last_body(*refs, taps=taps, shift=shift_of(layers - 1), nparts=len(parts), nw=len(weights)):
        ins = refs[: nparts + nw + 1]
        sig, part, gpart, fac_f, fac_g, acc = refs[nparts + nw + 1 :]
        blocks = make_blocks(ins[nparts : nparts + nw], taps)
        sig[...] = total(ins[:nparts])
        forward_part(blocks, sig, shift, fac_f, fac_g, part, acc)
        backward_part(blocks, ins[-1], shift, fac_f, fac_g, gpart, acc)

    elems = sum(w.size for w in weights)
    last_scratch = [pltpu.VMEM((chan_count, m, half), f32)] * 2 + scratch
    sig, part, gpart = call(
        last_body, [*parts, *weights, grad], [act, act, act], last_scratch, m, elems, 2, "layer_last"
    )

    def of_group(values, which):
        values = values.reshape(tm_count, 2, take, width)
        return lax.dynamic_index_in_dim(values, which, 1, keepdims=False)

    def summed(base, partial):
        arrived = swap(of_group(partial, 1 - group))
        mine = of_group(partial, group).astype(f32) + arrived.astype(f32)
        return (of_group(base, group).astype(f32) + mine).astype(bf16)

    output = summed(sig, part)
    parts = [grad, gpart, swap(gpart)]
    for layer in reversed(range(layers - 1)):
        taps, weights = gathered[layer]
        fac_f, fac_g = factors[layer]

        def body(*refs, taps=taps, shift=shift_of(layer), nw=len(weights)):
            ins, (now, part, acc) = refs[: 5 + nw], refs[5 + nw :]
            now[...] = total(ins[:3])
            backward_part(make_blocks(ins[5:], taps), now, shift, ins[3], ins[4], part, acc)

        elems = sum(w.size for w in weights)
        now, part = call(
            body, [*parts, fac_f, fac_g, *weights], [act, act], scratch, m, elems, 1, "layer_backward"
        )
        if layer:
            parts = [now, part, swap(part)]
    input_grad = summed(now, part)

    back = jnp.stack([output, input_grad]).reshape(2, tm_count, take, chan_count, nb)
    back = back.transpose(1, 3, 0, 2, 4).reshape(peers, 2, take, nb)
    back = lax.all_to_all(back, BOTH, split_axis=0, concat_axis=0, tiled=True)
    back = back.transpose(1, 0, 2, 3).reshape(2, padded, nb)[:, :rows]
    return back[0], back[1]


def solution(mesh):
    return jax.shard_map(
        local,
        mesh=mesh,
        in_specs=(
            P(("groups", "tm"), "chan"),
            P(("groups", "tm"), "chan"),
            P(None, None, "tm", "chan"),
            P(None, None, "tm", "chan"),
            P(None, "chan", "tm"),
        ),
        out_specs=(P(("groups", "tm"), "chan"), P(("groups", "tm"), "chan")),
        check_vma=False,
    )
```

```python
import jax
import jax.numpy as jnp
from jax import lax
from jax.experimental import pallas as pl
from jax.experimental.pallas import tpu as pltpu
from jax.sharding import PartitionSpec as P

BOTH = ("tm", "chan")
STAGES = ((0, 1), (2, 3))


def dot(left, right):
    return jnp.dot(left, right, preferred_element_type=jnp.float32)


def dot_t(left, right):
    return lax.dot_general(
        left, right, (((1,), (1,)), ((), ())), preferred_element_type=jnp.float32
    )


def exchange(values, axis, bit):
    return lax.ppermute(values, axis, [(i, i ^ bit) for i in range(lax.axis_size(axis))])


def bits_of(axis, least):
    return [1 << b for b in range(10) if least <= 1 << b < lax.axis_size(axis)]


class Piece:
    def __init__(self, array, keys, kind):
        self.array, self.keys, self.kind = array, keys, kind

    def moved(self, axis, bit):
        place = 0 if axis == "chan" else 1
        keys = [tuple(o ^ (bit if n == place else 0) for n, o in enumerate(k)) for k in self.keys]
        return Piece(exchange(self.array, axis, bit), keys, self.kind)


def merged(pieces, limit):
    if len(pieces) <= limit:
        return pieces
    joined = []
    for kind in ("full", "mine", "other"):
        same = [p for p in pieces if p.kind == kind]
        if same:
            array = jnp.concatenate([p.array for p in same], axis=0)
            joined.append(Piece(array, sum((p.keys for p in same), []), kind))
    return joined


def spread(own, group):
    limit = 16
    rows = own.shape[1]
    half = lax.dynamic_slice_in_dim(own, group * (rows // 2), rows // 2, 1)
    full = [Piece(own[None], [(0, 0)], "full")]
    mine = [Piece(half[None], [(0, 0)], "mine")]
    for bit in bits_of("chan", 2):
        mine = merged(mine + [p.moved("chan", bit) for p in mine], limit // 4)
    mine_parts = []
    for p in mine:
        if (0, 0) in p.keys:
            at = [n for n, k in enumerate(p.keys) if k != (0, 0)]
            if at:
                array = jnp.stack([p.array[n] for n in at])
                mine_parts.append(Piece(array, [p.keys[n] for n in at], "mine"))
        else:
            mine_parts.append(p)
    mine = mine_parts
    for bit in bits_of("tm", 2):
        full = merged(full + [p.moved("tm", bit) for p in full], limit // 4)
        mine = merged(mine + [p.moved("tm", bit) for p in mine], limit // 4)
    other = [
        Piece(exchange(p.array, "groups", 1), p.keys, "other") for p in mine
    ]
    pieces = full + mine + other
    if lax.axis_size("tm") > 1:
        pieces = pieces + [p.moved("tm", 1) for p in pieces]
    return merged(pieces, limit)


class Blocks:
    def __init__(self, refs, pieces, at, scratch, sems, panels, taps, kb, square):
        self.scratch, self.panels, self.taps, self.kb = scratch, panels, taps, kb
        self.square = square
        self.nb = scratch.shape[2]
        self.kblocks = scratch.shape[0] // panels
        self.copies = [[] for _ in range(panels)]
        group = lax.axis_index("groups")
        rows = scratch.shape[1]
        number = 0
        for ref, (keys, kind) in zip(refs, pieces):
            for lead, (dz, dtm) in enumerate(keys):
                target = scratch.at[dz // 2 * self.kblocks + dtm]
                if kind != "full":
                    which = group if kind == "mine" else 1 - group
                    start = pl.multiple_of(which * (rows // 2), rows // 2)
                    target = target.at[pl.ds(start, rows // 2)]
                copy = pltpu.make_async_copy(ref.at[lead, at], target, sems.at[number])
                self.copies[dz // 2].append(copy)
                number += 1

    def start(self):
        for copies in self.copies:
            for copy in copies:
                copy.start()

    def wait(self, panel):
        for copy in self.copies[panel]:
            copy.wait()

    def mat(self, which, panel, i):
        return self.scratch[panel * self.kblocks + i, pl.ds(which * self.kb, self.kb), :]

    def filt(self, tap, panel, i):
        return self.mat(tap, panel, i)

    def gate(self, tap, panel, i):
        return self.mat(self.taps + tap, panel, i)

    def mixed(self, gated, panel, i):
        mix = self.mat(2 * self.taps, panel, i)
        return dot(gated, mix) if self.square else dot_t(gated, mix)

    def unmixed(self, grad, panel, i):
        mix = self.mat(2 * self.taps, panel, i)
        return dot_t(grad, mix) if self.square else dot(grad, mix)


def down(values, rows):
    return jnp.concatenate([jnp.zeros_like(values[:rows]), values[: values.shape[0] - rows]], axis=0)


def up(values, rows):
    return jnp.concatenate([values[rows:], jnp.zeros_like(values[:rows])], axis=0)


def total(parts):
    if len(parts) == 1:
        return parts[0][...]
    base, own, other = (part[...].astype(jnp.float32) for part in parts)
    return (base + (own + other)).astype(jnp.bfloat16)


def add_to(acc_ref, cols, term, first):
    if first:
        acc_ref[:, cols] = term
    else:
        acc_ref[:, cols] += term


def forward_part(blocks, x_ref, shift, fac_f, fac_g, part_ref, acc_ref, waits=True):
    kb, taps = blocks.kb, blocks.taps
    for panel in range(blocks.panels):
        if waits:
            blocks.wait(panel)
        sums = []
        for kernel in (blocks.filt, blocks.gate):
            pre = None
            for tap in range(taps):
                value = None
                for i in range(blocks.kblocks):
                    term = dot(x_ref[:, pl.ds(i * kb, kb)], kernel(tap, panel, i))
                    value = term if value is None else value + term
                if tap < taps - 1:
                    value = down(value, shift)
                pre = value if pre is None else pre + value
            sums.append(pre)
        tanh_value = jnp.tanh(sums[0])
        sig_value = jax.nn.sigmoid(sums[1])
        gated = (tanh_value * sig_value).astype(jnp.bfloat16)
        fac_f[panel] = sig_value * (1.0 - tanh_value * tanh_value)
        fac_g[panel] = tanh_value * sig_value * (1.0 - sig_value)
        for i in range(blocks.kblocks):
            add_to(acc_ref, pl.ds(i * kb, kb), blocks.mixed(gated, panel, i), panel == 0)
    part_ref[...] = acc_ref[...].astype(jnp.bfloat16)


def backward_part(blocks, g_ref, shift, fac_f, fac_g, part_ref, acc_ref, waits=True):
    kb, taps = blocks.kb, blocks.taps
    for panel in range(blocks.panels):
        if waits:
            blocks.wait(panel)
        grad_z = None
        for i in range(blocks.kblocks):
            term = blocks.unmixed(g_ref[:, pl.ds(i * kb, kb)], panel, i)
            grad_z = term if grad_z is None else grad_z + term
        grad_f = (grad_z * fac_f[panel]).astype(jnp.bfloat16)
        grad_g = (grad_z * fac_g[panel]).astype(jnp.bfloat16)
        for i in range(blocks.kblocks):
            near = None
            for tap in range(taps):
                term = dot_t(grad_f, blocks.filt(tap, panel, i))
                term = term + dot_t(grad_g, blocks.gate(tap, panel, i))
                if tap < taps - 1:
                    term = up(term, shift)
                near = term if near is None else near + term
            add_to(acc_ref, pl.ds(i * kb, kb), near, panel == 0)
    part_ref[...] = acc_ref[...].astype(jnp.bfloat16)


def flipped(values, index, count, block):
    shape = values.shape
    for bit in [1 << b for b in range(10) if 1 << b < count]:
        split = values.reshape(*shape[:-1], count // (2 * bit), 2, bit * block)
        values = jnp.where((index & bit) != 0, split[..., ::-1, :], split).reshape(shape)
    return values


def local(records, cotangent, filter_weight, gate_weight, mix_weight):
    layers = filter_weight.shape[0]
    rows, nb = records.shape
    kb = filter_weight.shape[2]
    tm_count, chan_count = lax.axis_size("tm"), lax.axis_size("chan")
    group, tm_index = lax.axis_index("groups"), lax.axis_index("tm")
    side = lax.axis_index("chan") % 2
    peers = tm_count * chan_count
    panels = chan_count // 2
    width = nb * chan_count
    bf16, f32 = jnp.bfloat16, jnp.float32
    square = kb == nb

    take = -(-rows // (4 * peers)) * 4
    padded = take * peers

    taps_of = [2 if 2**layer < tm_count else 1 for layer in range(layers)]
    weights_of = {}
    for stage in STAGES:
        packs = []
        for layer in stage:
            taps = taps_of[layer]
            mix = mix_weight[layer] if square else mix_weight[layer].T
            mats = [filter_weight[layer, t] for t in range(2 - taps, 2)]
            mats += [gate_weight[layer, t] for t in range(2 - taps, 2)]
            packs.append(jnp.concatenate(mats + [mix], axis=0))
        if len({p.shape[0] for p in packs}) > 1:
            for layer, pack in zip(stage, packs):
                weights_of[layer] = (spread(pack[None], group), 0)
        else:
            pieces = spread(jnp.stack(packs), group)
            for at, layer in enumerate(stage):
                weights_of[layer] = (pieces, at)

    def swap(values):
        return exchange(values, "chan", 1)

    both = jnp.pad(jnp.stack([records, cotangent]), ((0, 0), (0, padded - rows), (0, 0)))
    sent = both.reshape(2, peers, take, nb).transpose(1, 0, 2, 3)
    got = lax.all_to_all(sent, BOTH, split_axis=0, concat_axis=0, tiled=True)
    got = got.reshape(tm_count, chan_count, 2, take, nb).transpose(2, 0, 3, 1, 4)
    own = flipped(got.reshape(2, tm_count, take, width), tm_index, tm_count, kb)
    other = swap(own)
    first, second = jnp.where(side == 0, own, other), jnp.where(side == 0, other, own)
    pair = jnp.concatenate([first, second], axis=2)
    m = tm_count * 2 * take
    signal, grad = pair.reshape(2, m, width)

    vmem = pl.BlockSpec(memory_space=pltpu.VMEM)
    anywhere = pl.BlockSpec(memory_space=pl.ANY)
    act = jax.ShapeDtypeStruct((m, width), bf16)
    fac = jax.ShapeDtypeStruct((panels, m, nb), f32)

    def layer_call(layer, body, arrays, outs, scratch, passes, name):
        pieces, at = weights_of[layer]
        taps = taps_of[layer]
        shift = 2**layer * 2 * take
        height = pieces[0].array.shape[2]
        copies = sum(len(p.keys) for p in pieces)
        plan = [(p.keys, p.kind) for p in pieces]
        elems = panels * tm_count * height * nb

        def kernel(*refs):
            ins, refs = refs[: len(arrays)], refs[len(arrays) :]
            piece_refs, refs = refs[: len(pieces)], refs[len(pieces) :]
            held, sems = refs[-2:]
            blocks = Blocks(piece_refs, plan, at, held, sems, panels, taps, kb, square)
            blocks.start()
            body(blocks, shift, ins, refs[: len(outs)], refs[len(outs) : -2])

        return pl.pallas_call(
            kernel,
            out_shape=outs,
            in_specs=[vmem] * len(arrays) + [anywhere] * len(pieces),
            out_specs=[vmem] * len(outs),
            scratch_shapes=[
                *scratch,
                pltpu.VMEM((panels * tm_count, height, nb), bf16),
                pltpu.SemaphoreType.DMA((copies,)),
            ],
            compiler_params=pltpu.CompilerParams(vmem_limit_bytes=32 * 1024 * 1024),
            cost_estimate=pl.CostEstimate(
                flops=2 * m * elems * passes, bytes_accessed=2 * elems, transcendentals=2 * m * nb
            ),
            name=name,
        )(*arrays, *[p.array for p in pieces])

    acc = [pltpu.VMEM((m, width), f32)]

    def forward_body(blocks, shift, ins, outs, scratch):
        sig, part, fac_f, fac_g = outs
        sig[...] = total(ins)
        forward_part(blocks, sig, shift, fac_f, fac_g, part, scratch[0])

    def last_body(blocks, shift, ins, outs, scratch):
        sig, part, gpart = outs
        fac_f, fac_g, acc_ref = scratch
        sig[...] = total(ins[:-1])
        forward_part(blocks, sig, shift, fac_f, fac_g, part, acc_ref)
        backward_part(blocks, ins[-1], shift, fac_f, fac_g, gpart, acc_ref, waits=False)

    def backward_body(blocks, shift, ins, outs, scratch):
        now, part = outs
        now[...] = total(ins[:3])
        backward_part(blocks, now, shift, ins[3], ins[4], part, scratch[0])

    factors = []
    parts = [signal]
    for layer in range(layers - 1):
        sig, part, fac_f, fac_g = layer_call(
            layer, forward_body, parts, [act, act, fac, fac], acc, 1, "layer_forward"
        )
        factors.append((fac_f, fac_g))
        parts = [sig, part, swap(part)]
    facs = [pltpu.VMEM((panels, m, nb), f32)] * 2
    sig, part, gpart = layer_call(
        layers - 1, last_body, [*parts, grad], [act, act, act], facs + acc, 2, "layer_last"
    )

    def of_side(values, which):
        values = values.reshape(tm_count, 2, take, width)
        return lax.dynamic_index_in_dim(values, which, 1, keepdims=False)

    def summed(base, partial):
        arrived = swap(of_side(partial, 1 - side))
        mine = of_side(partial, side).astype(f32) + arrived.astype(f32)
        return (of_side(base, side).astype(f32) + mine).astype(bf16)

    output = summed(sig, part)
    parts = [grad, gpart, swap(gpart)]
    for layer in reversed(range(layers - 1)):
        now, part = layer_call(
            layer, backward_body, [*parts, *factors[layer]], [act, act], acc, 1, "layer_backward"
        )
        if layer:
            parts = [now, part, swap(part)]
    input_grad = summed(now, part)

    back = flipped(jnp.stack([output, input_grad]), tm_index, tm_count, kb)
    back = back.reshape(2, tm_count, take, chan_count, nb)
    back = back.transpose(1, 3, 0, 2, 4).reshape(peers, 2, take, nb)
    back = lax.all_to_all(back, BOTH, split_axis=0, concat_axis=0, tiled=True)
    back = back.transpose(1, 0, 2, 3).reshape(2, padded, nb)[:, :rows]
    return back[0], back[1]


def solution(mesh):
    return jax.shard_map(
        local,
        mesh=mesh,
        in_specs=(
            P(("groups", "tm"), "chan"),
            P(("groups", "tm"), "chan"),
            P(None, None, "tm", "chan"),
            P(None, None, "tm", "chan"),
            P(None, "chan", "tm"),
        ),
        out_specs=(P(("groups", "tm"), "chan"), P(("groups", "tm"), "chan")),
        check_vma=False,
    )
```

```python
import jax
import jax.numpy as jnp
from jax import lax
from jax.experimental import pallas as pl
from jax.experimental.pallas import tpu as pltpu
from jax.sharding import PartitionSpec as P

BOTH = ("tm", "chan")
HALVED = (0, 2)
VMEM_LIMIT = 20 * 1024 * 1024


def dot(left, right):
    return jnp.dot(left, right, preferred_element_type=jnp.float32)


def dot_t(left, right):
    return lax.dot_general(
        left, right, (((1,), (1,)), ((), ())), preferred_element_type=jnp.float32
    )


def exchange(values, axis, bit):
    return lax.ppermute(values, axis, [(i, i ^ bit) for i in range(lax.axis_size(axis))])


def bits_of(axis, least):
    return [1 << b for b in range(10) if least <= 1 << b < lax.axis_size(axis)]


class Piece:
    def __init__(self, array, keys, kind):
        self.array, self.keys, self.kind = array, keys, kind

    def moved(self, axis, bit, kind=None):
        flip = {"chan": (bit, 0), "tm": (0, bit), "groups": (0, 0)}[axis]
        keys = [(k[0] ^ flip[0], k[1] ^ flip[1]) for k in self.keys]
        return Piece(exchange(self.array, axis, bit), keys, kind or self.kind)


def merged(pieces, limit):
    if len(pieces) <= limit:
        return pieces
    joined = []
    for kind in ("full", "mine", "other"):
        same = [p for p in pieces if p.kind == kind]
        if same:
            array = jnp.concatenate([p.array for p in same], axis=0)
            joined.append(Piece(array, sum((p.keys for p in same), []), kind))
    return joined


def doubled(pieces, axis, bits, limit):
    for bit in bits:
        pieces = merged(pieces + [p.moved(axis, bit) for p in pieces], limit)
    return pieces


def packed(sources, taps_of):
    kb, nb = sources[0].shape[2:]
    shapes = []
    for taps in taps_of:
        shapes += [(1, 2 * taps + 1, kb // 2, nb), (1, 2 * taps + 1, kb, nb)]

    def kernel(*refs):
        filt, gate, mix = refs[:3]
        outs, sems = refs[3:-1], refs[-1]
        copies = []
        for n, out in enumerate(outs):
            layer, taps, rows = n // 2, taps_of[n // 2], out.shape[2]
            start = lax.axis_index("groups") * rows if n % 2 == 0 else 0
            window = pl.ds(pl.multiple_of(start, rows), rows)
            for w, ref in enumerate((filt, gate)):
                source = ref.at[layer, pl.ds(2 - taps, taps), window]
                target = out.at[0, pl.ds(w * taps, taps)]
                copies.append(pltpu.make_async_copy(source, target, sems.at[n, w]))
            copies.append(
                pltpu.make_async_copy(mix.at[layer, window], out.at[0, 2 * taps], sems.at[n, 2])
            )
        for copy in copies:
            copy.start()
        for copy in copies:
            copy.wait()

    return pl.pallas_call(
        kernel,
        out_shape=[jax.ShapeDtypeStruct(shape, jnp.bfloat16) for shape in shapes],
        in_specs=[pl.BlockSpec(memory_space=pl.ANY)] * 3,
        out_specs=[pl.BlockSpec(memory_space=pltpu.VMEM)] * len(shapes),
        scratch_shapes=[pltpu.SemaphoreType.DMA((len(shapes), 3))],
        name="pack",
    )(*sources)


class Links:
    def __init__(self, depth):
        self.depth, self.sent = depth, {}

    def move(self, piece, axis, bit, kind=None, after=()):
        sent = self.sent.setdefault(axis, [])
        waits = [*after, *sent[-self.depth :][:1]] if len(sent) >= self.depth else [*after]
        if waits:
            piece.array = lax.optimization_barrier((piece.array, *waits))[0]
        moved = piece.moved(axis, bit, kind)
        sent.append(moved.array)
        return moved


def spread(packs, taps_of, halved_layers, links):
    limit = 16 if lax.axis_size("tm") <= 4 and lax.axis_size("chan") <= 4 else 1
    high = bits_of("tm", 2)
    layers = range(len(taps_of))
    halves = [Piece(packs[2 * n], [(0, 0)], "mine") for n in layers]
    full = [[Piece(packs[2 * n + 1], [(0, 0)], "full")] for n in layers]
    zs = [[] for _ in layers]
    ys = [[] for _ in layers]
    crossed = [[] for _ in layers]
    others = [[] for _ in layers]

    def along_chan(n):
        for bit in bits_of("chan", 2):
            zs[n] = zs[n] + [links.move(p, "chan", bit) for p in [halves[n]] + zs[n]]

    def own_along_tm(n):
        for bit in high:
            if n in halved_layers:
                ys[n] = ys[n] + [links.move(p, "tm", bit) for p in [halves[n]] + ys[n]]
            else:
                full[n] = full[n] + [links.move(p, "tm", bit) for p in full[n]]

    def others_along_tm(n):
        for bit in high:
            source = merged(zs[n] + crossed[n], limit)
            crossed[n] = crossed[n] + [links.move(p, "tm", bit) for p in source]

    def along_groups(n, pieces):
        others[n] = others[n] + [links.move(p, "groups", 1, "other") for p in merged(pieces, limit)]

    steps = [(along_chan, 0), (own_along_tm, 0), (own_along_tm, 1), (along_chan, 1)]
    for step, n in steps:
        step(n)
    for n in layers:
        along_groups(n, ys[n])
        others_along_tm(n)
        along_groups(n, zs[n])
        if n + 2 < len(taps_of):
            along_chan(n + 2)
            own_along_tm(n + 2)
        along_groups(n, crossed[n])
    result = []
    for n in layers:
        pieces = merged(full[n] + ys[n] + zs[n] + crossed[n] + others[n], limit)
        if lax.axis_size("tm") > 1:
            pieces = pieces + [p.moved("tm", 1) for p in pieces]
        result.append(pieces)
    return result


class Blocks:
    def __init__(self, held, panels, taps, square):
        self.held, self.panels, self.taps, self.square = held, panels, taps, square
        self.kblocks = held.shape[0] // panels
        self.kb = held.shape[2]
        self.copies = {}

    def fill(self, refs, plan, sems):
        group = lax.axis_index("groups")
        half = self.kb // 2
        number = 0
        for ref, (keys, kind) in zip(refs, plan):
            for lead, (dz, dtm) in enumerate(keys):
                target = self.held.at[dz // 2 * self.kblocks + dtm]
                if kind != "full":
                    which = group if kind == "mine" else 1 - group
                    window = pl.ds(pl.multiple_of(which * half, half), half)
                    target = self.held.at[dz // 2 * self.kblocks + dtm, :, window]
                copy = pltpu.make_async_copy(ref.at[lead], target, sems.at[number])
                self.copies.setdefault((dz // 2, dtm), []).append(copy)
                number += 1
        for panel in range(self.panels):
            for i in range(self.kblocks):
                for copy in self.copies[panel, i]:
                    copy.start()

    def wait(self, panel, i):
        for copy in self.copies.pop((panel, i), []):
            copy.wait()

    def mat(self, which, panel, i):
        return self.held[panel * self.kblocks + i, which]

    def filt(self, tap, panel, i):
        return self.mat(tap, panel, i)

    def gate(self, tap, panel, i):
        return self.mat(self.taps + tap, panel, i)

    def mixed(self, gated, panel, i):
        mix = self.mat(2 * self.taps, panel, i)
        return dot(gated, mix) if self.square else dot_t(gated, mix)

    def unmixed(self, grad, panel, i):
        mix = self.mat(2 * self.taps, panel, i)
        return dot_t(grad, mix) if self.square else dot(grad, mix)


def down(values, rows):
    return jnp.concatenate([jnp.zeros_like(values[:rows]), values[: values.shape[0] - rows]], axis=0)


def up(values, rows):
    return jnp.concatenate([values[rows:], jnp.zeros_like(values[:rows])], axis=0)


def total(parts):
    if len(parts) == 1:
        return parts[0][...]
    base, own, other = (part[...].astype(jnp.float32) for part in parts)
    return (base + (own + other)).astype(jnp.bfloat16)


def add_to(acc_ref, cols, term, first):
    if first:
        acc_ref[:, cols] = term
    else:
        acc_ref[:, cols] += term


def forward_part(blocks, x_ref, shift, fac_f, fac_g, acc_ref):
    kb, taps = blocks.kb, blocks.taps
    for panel in range(blocks.panels):
        sums = [[None] * taps, [None] * taps]
        for i in range(blocks.kblocks):
            blocks.wait(panel, i)
            x = x_ref[:, pl.ds(i * kb, kb)]
            for n, kernel in enumerate((blocks.filt, blocks.gate)):
                for tap in range(taps):
                    term = dot(x, kernel(tap, panel, i))
                    sums[n][tap] = term if i == 0 else sums[n][tap] + term
        pre = [s[-1] if taps == 1 else s[-1] + down(s[0], shift) for s in sums]
        tanh_value = jnp.tanh(pre[0])
        sig_value = jax.nn.sigmoid(pre[1])
        gated = (tanh_value * sig_value).astype(jnp.bfloat16)
        fac_f[panel] = sig_value * (1.0 - tanh_value * tanh_value)
        fac_g[panel] = tanh_value * sig_value * (1.0 - sig_value)
        for i in range(blocks.kblocks):
            add_to(acc_ref, pl.ds(i * kb, kb), blocks.mixed(gated, panel, i), panel == 0)


def backward_part(blocks, g_ref, shift, fac_f, fac_g, acc_ref):
    kb, taps = blocks.kb, blocks.taps
    for panel in range(blocks.panels):
        grad_z = None
        for i in range(blocks.kblocks):
            term = blocks.unmixed(g_ref[:, pl.ds(i * kb, kb)], panel, i)
            grad_z = term if grad_z is None else grad_z + term
        grad_f = (grad_z * fac_f[panel]).astype(jnp.bfloat16)
        grad_g = (grad_z * fac_g[panel]).astype(jnp.bfloat16)
        for i in range(blocks.kblocks):
            near = None
            for tap in range(taps):
                term = dot_t(grad_f, blocks.filt(tap, panel, i))
                term = term + dot_t(grad_g, blocks.gate(tap, panel, i))
                if tap < taps - 1:
                    term = up(term, shift)
                near = term if near is None else near + term
            add_to(acc_ref, pl.ds(i * kb, kb), near, panel == 0)


def flipped(values, index, count, block):
    shape = values.shape
    for bit in [1 << b for b in range(10) if 1 << b < count]:
        split = values.reshape(*shape[:-1], count // (2 * bit), 2, bit * block)
        values = jnp.where((index & bit) != 0, split[..., ::-1, :], split).reshape(shape)
    return values


def local(records, cotangent, filter_weight, gate_weight, mix_weight):
    layers = filter_weight.shape[0]
    rows, nb = records.shape
    kb = filter_weight.shape[2]
    tm_count, chan_count = lax.axis_size("tm"), lax.axis_size("chan")
    tm_index = lax.axis_index("tm")
    peers = tm_count * chan_count
    panels = chan_count // 2
    width = nb * chan_count
    bf16, f32 = jnp.bfloat16, jnp.float32
    square = kb == nb

    span = -(-rows // (4 * peers)) * 8
    padded = span * peers // 2
    m = tm_count * span

    taps_of = [2 if 2**layer < tm_count else 1 for layer in range(layers)]
    mix_source = mix_weight if square else mix_weight.transpose(0, 2, 1)
    sources = (filter_weight, gate_weight, mix_source)
    pieces_of = spread(packed(sources, taps_of), taps_of, HALVED, Links(2))

    def swap(values):
        return exchange(values, "chan", 1)

    both = jnp.pad(jnp.stack([records, cotangent]), ((0, 0), (0, padded - rows), (0, 0)))
    sent = both.reshape(2, peers // 2, span, nb).transpose(1, 0, 2, 3)
    sent = jnp.broadcast_to(sent[:, None], (peers // 2, 2, 2, span, nb)).reshape(peers, 2, span, nb)
    got = lax.all_to_all(sent, BOTH, split_axis=0, concat_axis=0, tiled=True)
    if not square:
        got = got.reshape(tm_count, chan_count, 2, span, nb).transpose(2, 0, 3, 1, 4)
        got = flipped(got.reshape(2, tm_count, span, width), tm_index, tm_count, kb)
        got = got.reshape(2, tm_count, span, tm_count, kb).transpose(1, 3, 0, 2, 4)
        got = got.reshape(tm_count * tm_count, 2, span, kb)

    def place(s, i):
        return s * tm_count + ((i ^ lax.axis_index("tm")) if square else i)

    def assemble(got_ref, which, target):
        for i in range(tm_count):
            parts = [got_ref[place(s, i), which].astype(f32) for s in range(tm_count)]
            target[:, pl.ds(i * kb, kb)] = jnp.concatenate(parts, axis=0).astype(bf16)

    vmem = pl.BlockSpec(memory_space=pltpu.VMEM)
    anywhere = pl.BlockSpec(memory_space=pl.ANY)
    act = jax.ShapeDtypeStruct((m, width), bf16)
    fac = jax.ShapeDtypeStruct((panels, m, nb), f32)
    acc = [pltpu.VMEM((m, width), f32)]

    def layer_call(layer, body, arrays, held, outs, scratch, passes, name):
        taps, mats = taps_of[layer], 2 * taps_of[layer] + 1
        shift = 2**layer * span
        pieces = pieces_of[layer] if held is None else []
        copies = sum(len(p.keys) for p in pieces)
        plan = [(p.keys, p.kind) for p in pieces]
        shape = (panels * tm_count, mats, kb, nb)
        elems = panels * tm_count * mats * kb * nb
        count = len(arrays)

        def kernel(*refs):
            ins, refs = refs[:count], refs[count:]
            if held is None:
                piece_refs, refs = refs[: len(pieces)], refs[len(pieces) :]
                blocks = Blocks(refs[len(outs)], panels, taps, square)
                blocks.fill(piece_refs, plan, refs[-1])
                body(blocks, shift, ins, refs[: len(outs)], refs[len(outs) + 1 : -1])
            else:
                blocks = Blocks(refs[0], panels, taps, square)
                body(blocks, shift, ins, refs[1 : 1 + len(outs)], refs[1 + len(outs) :])

        filling = held is None
        weights = [p.array for p in pieces] if filling else [held]
        return pl.pallas_call(
            kernel,
            out_shape=[*outs, *([jax.ShapeDtypeStruct(shape, bf16)] if filling else [])],
            in_specs=[vmem] * count + [anywhere if filling else vmem] * len(weights),
            out_specs=[vmem] * (len(outs) + filling),
            scratch_shapes=[*scratch, *([pltpu.SemaphoreType.DMA((copies,))] if filling else [])],
            compiler_params=pltpu.CompilerParams(vmem_limit_bytes=VMEM_LIMIT),
            cost_estimate=pl.CostEstimate(
                flops=2 * m * elems * passes, bytes_accessed=2 * elems, transcendentals=2 * m * nb
            ),
            name=name,
        )(*arrays, *weights)

    def first_body(blocks, shift, ins, outs, scratch):
        sig, grad, part, fac_f, fac_g = outs
        assemble(ins[0], 0, sig)
        assemble(ins[0], 1, grad)
        forward_part(blocks, sig, shift, fac_f, fac_g, scratch[0])
        part[...] = scratch[0][...].astype(bf16)

    def forward_body(blocks, shift, ins, outs, scratch):
        sig, part, fac_f, fac_g = outs
        sig[...] = total(ins)
        forward_part(blocks, sig, shift, fac_f, fac_g, scratch[0])
        part[...] = scratch[0][...].astype(bf16)

    def last_body(blocks, shift, ins, outs, scratch):
        sig, part, gpart = outs
        fac_f, fac_g, acc_ref = scratch
        sig[...] = total(ins[:-1])
        forward_part(blocks, sig, shift, fac_f, fac_g, acc_ref)
        part[...] = acc_ref[...].astype(bf16)
        backward_part(blocks, ins[-1], shift, fac_f, fac_g, acc_ref)
        gpart[...] = acc_ref[...].astype(bf16)

    def backward_body(blocks, shift, ins, outs, scratch):
        now, part = outs
        now[...] = total(ins[:3])
        backward_part(blocks, now, shift, ins[3], ins[4], scratch[0])
        part[...] = scratch[0][...].astype(bf16)

    def final_body(blocks, shift, ins, outs, scratch):
        acc_ref, now = scratch
        now[...] = total(ins[:3])
        backward_part(blocks, now, shift, ins[3], ins[4], acc_ref)
        even = lax.axis_index("chan") % 2 == 0
        for i in range(tm_count):
            cols = pl.ds(i * kb, kb)
            base = now[:, cols].astype(f32)
            value = acc_ref[:, cols] + jnp.where(even, base, jnp.zeros_like(base))
            out = sum(ins[n][:, cols].astype(f32) for n in (6, 7)) + ins[5][:, cols].astype(f32)
            if square:
                out = jnp.where(even, out[:, : kb // 2], out[:, kb // 2 :])
            for s in range(tm_count):
                part = slice(s * span, (s + 1) * span)
                outs[0][place(s, i), :, :kb] = value[part].astype(bf16)
                outs[0][place(s, i), :, kb:] = out[part].astype(bf16)

    factors, helds = [], []
    sig, grad, part, fac_f, fac_g, held = layer_call(
        0, first_body, [got], None, [act, act, act, fac, fac], acc, 1, "layer_first"
    )
    for layer in range(1, layers - 1):
        factors.append((fac_f, fac_g))
        helds.append(held)
        sig, part, fac_f, fac_g, held = layer_call(
            layer, forward_body, [sig, part, swap(part)], None, [act, act, fac, fac], acc, 1, "layer_forward"
        )
    factors.append((fac_f, fac_g))
    helds.append(held)
    facs = [pltpu.VMEM((panels, m, nb), f32)] * 2
    sig, part, gpart, _ = layer_call(
        layers - 1,
        last_body,
        [sig, part, swap(part), grad],
        None,
        [act, act, act],
        facs + acc,
        2,
        "layer_last",
    )
    parts = [grad, gpart, swap(gpart)]
    output = [sig, part, swap(part)]
    for layer in reversed(range(1, layers - 1)):
        now, gpart = layer_call(
            layer,
            backward_body,
            [*parts, *factors[layer]],
            helds[layer],
            [act, act],
            acc,
            1,
            "layer_backward",
        )
        parts = [now, gpart, swap(gpart)]

    extra = kb // 2 if square else kb
    leaving = jax.ShapeDtypeStruct((tm_count * tm_count, span, kb + extra), bf16)
    back = layer_call(
        0,
        final_body,
        [*parts, *factors[0], *output],
        helds[0],
        [leaving],
        [*acc, pltpu.VMEM((m, width), bf16)],
        1,
        "layer_final",
    )[0]
    if not square:

        def regrouped(values):
            values = values.reshape(tm_count, tm_count, span, kb).transpose(0, 2, 1, 3)
            values = flipped(values.reshape(tm_count, span, width), tm_index, tm_count, kb)
            values = values.reshape(tm_count, span, chan_count, nb).transpose(0, 2, 1, 3)
            return values.reshape(peers, span, nb)

        out = regrouped(back[..., kb:])
        out = jnp.where(lax.axis_index("chan") % 2 == 0, out[..., : nb // 2], out[..., nb // 2 :])
        back = jnp.concatenate([regrouped(back[..., :kb]), out], axis=-1)
    back = lax.all_to_all(back, BOTH, split_axis=0, concat_axis=0, tiled=True)
    back = back.reshape(peers // 2, 2, span, nb + nb // 2)
    grads = back[..., :nb].astype(f32)
    input_grad = (grads[:, 0] + grads[:, 1]).astype(bf16).reshape(padded, nb)[:rows]
    output = jnp.concatenate([back[:, 0, :, nb:], back[:, 1, :, nb:]], axis=-1)
    return output.reshape(padded, nb)[:rows], input_grad


def solution(mesh):
    return jax.shard_map(
        local,
        mesh=mesh,
        in_specs=(
            P(("groups", "tm"), "chan"),
            P(("groups", "tm"), "chan"),
            P(None, None, "tm", "chan"),
            P(None, None, "tm", "chan"),
            P(None, "chan", "tm"),
        ),
        out_specs=(P(("groups", "tm"), "chan"), P(("groups", "tm"), "chan")),
        check_vma=False,
    )
```

```python
import jax
import jax.numpy as jnp
from jax import lax
from jax.experimental import pallas as pl
from jax.experimental.pallas import tpu as pltpu
from jax.sharding import PartitionSpec as P

BOTH = ("tm", "chan")
HALVED = (0, 2)
VMEM_LIMIT = 20 * 1024 * 1024
DEPTHS = {"chan": 1, "tm": 2, "groups": 2}


def dot(left, right):
    return jnp.dot(left, right, preferred_element_type=jnp.float32)


def dot_t(left, right):
    return lax.dot_general(
        left, right, (((1,), (1,)), ((), ())), preferred_element_type=jnp.float32
    )


def exchange(values, axis, bit):
    return lax.ppermute(values, axis, [(i, i ^ bit) for i in range(lax.axis_size(axis))])


def bits_of(axis, least):
    return [1 << b for b in range(10) if least <= 1 << b < lax.axis_size(axis)]


class Piece:
    def __init__(self, array, keys, kind):
        self.array, self.keys, self.kind = array, keys, kind

    def moved(self, axis, bit, kind=None):
        flip = {"chan": (bit, 0), "tm": (0, bit), "groups": (0, 0)}[axis]
        keys = [(k[0] ^ flip[0], k[1] ^ flip[1]) for k in self.keys]
        return Piece(exchange(self.array, axis, bit), keys, kind or self.kind)


def merged(pieces, limit):
    if len(pieces) <= limit:
        return pieces
    joined = []
    for kind in ("full", "mine", "other"):
        same = [p for p in pieces if p.kind == kind]
        if same:
            array = jnp.concatenate([p.array for p in same], axis=0)
            joined.append(Piece(array, sum((p.keys for p in same), []), kind))
    return joined


def doubled(pieces, axis, bits, limit):
    for bit in bits:
        pieces = merged(pieces + [p.moved(axis, bit) for p in pieces], limit)
    return pieces


def packed(sources, taps_of):
    kb, nb = sources[0].shape[2:]
    shapes = []
    for taps in taps_of:
        shapes += [(1, 2 * taps + 1, kb // 2, nb), (1, 2 * taps + 1, kb, nb)]

    def kernel(*refs):
        filt, gate, mix = refs[:3]
        outs, sems = refs[3:-1], refs[-1]
        copies = []
        for n, out in enumerate(outs):
            layer, taps, rows = n // 2, taps_of[n // 2], out.shape[2]
            start = lax.axis_index("groups") * rows if n % 2 == 0 else 0
            window = pl.ds(pl.multiple_of(start, rows), rows)
            for w, ref in enumerate((filt, gate)):
                source = ref.at[layer, pl.ds(2 - taps, taps), window]
                target = out.at[0, pl.ds(w * taps, taps)]
                copies.append(pltpu.make_async_copy(source, target, sems.at[n, w]))
            copies.append(
                pltpu.make_async_copy(mix.at[layer, window], out.at[0, 2 * taps], sems.at[n, 2])
            )
        for copy in copies:
            copy.start()
        for copy in copies:
            copy.wait()

    return pl.pallas_call(
        kernel,
        out_shape=[jax.ShapeDtypeStruct(shape, jnp.bfloat16) for shape in shapes],
        in_specs=[pl.BlockSpec(memory_space=pl.ANY)] * 3,
        out_specs=[pl.BlockSpec(memory_space=pltpu.VMEM)] * len(shapes),
        scratch_shapes=[pltpu.SemaphoreType.DMA((len(shapes), 3))],
        name="pack",
    )(*sources)


class Links:
    def __init__(self, depths):
        self.depths, self.sent = depths, {}

    def move(self, piece, axis, bit, kind=None, after=()):
        sent, depth = self.sent.setdefault(axis, []), self.depths[axis]
        waits = [*after, *(sent[-depth:][:1] if len(sent) >= depth else [])]
        if waits:
            piece.array = lax.optimization_barrier((piece.array, *waits))[0]
        moved = piece.moved(axis, bit, kind)
        sent.append(moved.array)
        return moved


class Weights:
    def __init__(self, packs, taps_of, halved, depths):
        self.limit = 16 if lax.axis_size("tm") <= 4 and lax.axis_size("chan") <= 4 else 1
        self.links, self.halved, self.high = Links(depths), halved, bits_of("tm", 2)
        count = len(taps_of)
        self.halves = [Piece(packs[2 * n], [(0, 0)], "mine") for n in range(count)]
        self.full = [[Piece(packs[2 * n + 1], [(0, 0)], "full")] for n in range(count)]
        self.zs, self.ys, self.crossed, self.others = ([[] for _ in range(count)] for _ in range(4))

    def along_chan(self, n, after=()):
        for bit in bits_of("chan", 2):
            sources = [self.halves[n]] + self.zs[n]
            self.zs[n] = self.zs[n] + [self.links.move(p, "chan", bit, None, after) for p in sources]

    def own_along_tm(self, n, after=()):
        for bit in self.high:
            if n in self.halved:
                sources = [self.halves[n]] + self.ys[n]
                self.ys[n] = self.ys[n] + [self.links.move(p, "tm", bit, None, after) for p in sources]
            else:
                moved = [self.links.move(p, "tm", bit, None, after) for p in self.full[n]]
                self.full[n] = self.full[n] + moved

    def others_along_tm(self, n, after=()):
        for bit in self.high:
            sources = merged(self.zs[n] + self.crossed[n], self.limit)
            self.crossed[n] = self.crossed[n] + [
                self.links.move(p, "tm", bit, None, after) for p in sources
            ]

    def along_groups(self, n, pieces, after=()):
        for p in merged(pieces, self.limit):
            self.others[n].append(self.links.move(p, "groups", 1, "other", after))

    def begin(self, after):
        self.along_chan(0)
        self.own_along_tm(0)
        self.own_along_tm(1)
        self.along_chan(1, after)

    def layer(self, n, after=()):
        self.along_groups(n, self.ys[n])
        self.others_along_tm(n)
        self.along_groups(n, self.zs[n])
        if n + 2 < len(self.full):
            self.along_chan(n + 2)
            self.own_along_tm(n + 2, after)
        self.along_groups(n, self.crossed[n])
        pieces = merged(
            self.full[n] + self.ys[n] + self.zs[n] + self.crossed[n] + self.others[n], self.limit
        )
        if lax.axis_size("tm") > 1:
            pieces = pieces + [p.moved("tm", 1) for p in pieces]
        return pieces


class Blocks:
    def __init__(self, held, panels, taps, square):
        self.held, self.panels, self.taps, self.square = held, panels, taps, square
        self.kblocks = held.shape[0] // panels
        self.kb = held.shape[2]
        self.copies = {}

    def fill(self, refs, plan, sems):
        group = lax.axis_index("groups")
        half = self.kb // 2
        number = 0
        for ref, (keys, kind) in zip(refs, plan):
            for lead, (dz, dtm) in enumerate(keys):
                target = self.held.at[dz // 2 * self.kblocks + dtm]
                if kind != "full":
                    which = group if kind == "mine" else 1 - group
                    window = pl.ds(pl.multiple_of(which * half, half), half)
                    target = self.held.at[dz // 2 * self.kblocks + dtm, :, window]
                copy = pltpu.make_async_copy(ref.at[lead], target, sems.at[number])
                self.copies.setdefault((dz // 2, dtm), []).append(copy)
                number += 1
        for panel in range(self.panels):
            for i in range(self.kblocks):
                for copy in self.copies[panel, i]:
                    copy.start()

    def wait(self, panel, i):
        for copy in self.copies.pop((panel, i), []):
            copy.wait()

    def mat(self, which, panel, i):
        return self.held[panel * self.kblocks + i, which]

    def filt(self, tap, panel, i):
        return self.mat(tap, panel, i)

    def gate(self, tap, panel, i):
        return self.mat(self.taps + tap, panel, i)

    def mixed(self, gated, panel, i):
        mix = self.mat(2 * self.taps, panel, i)
        return dot(gated, mix) if self.square else dot_t(gated, mix)

    def unmixed(self, grad, panel, i):
        mix = self.mat(2 * self.taps, panel, i)
        return dot_t(grad, mix) if self.square else dot(grad, mix)


def down(values, rows):
    return jnp.concatenate([jnp.zeros_like(values[:rows]), values[: values.shape[0] - rows]], axis=0)


def up(values, rows):
    return jnp.concatenate([values[rows:], jnp.zeros_like(values[:rows])], axis=0)


def total(parts):
    if len(parts) == 1:
        return parts[0][...]
    base, own, other = (part[...].astype(jnp.float32) for part in parts)
    return (base + (own + other)).astype(jnp.bfloat16)


def add_to(acc_ref, cols, term, first):
    if first:
        acc_ref[:, cols] = term
    else:
        acc_ref[:, cols] += term


def forward_part(blocks, x_ref, shift, fac_f, fac_g, acc_ref):
    kb, taps = blocks.kb, blocks.taps
    for panel in range(blocks.panels):
        sums = [[None] * taps, [None] * taps]
        for i in range(blocks.kblocks):
            blocks.wait(panel, i)
            x = x_ref[:, pl.ds(i * kb, kb)]
            for n, kernel in enumerate((blocks.filt, blocks.gate)):
                for tap in range(taps):
                    term = dot(x, kernel(tap, panel, i))
                    sums[n][tap] = term if i == 0 else sums[n][tap] + term
        pre = [s[-1] if taps == 1 else s[-1] + down(s[0], shift) for s in sums]
        tanh_value = jnp.tanh(pre[0])
        sig_value = jax.nn.sigmoid(pre[1])
        gated = (tanh_value * sig_value).astype(jnp.bfloat16)
        fac_f[panel] = sig_value * (1.0 - tanh_value * tanh_value)
        fac_g[panel] = tanh_value * sig_value * (1.0 - sig_value)
        for i in range(blocks.kblocks):
            add_to(acc_ref, pl.ds(i * kb, kb), blocks.mixed(gated, panel, i), panel == 0)


def backward_part(blocks, g_ref, shift, fac_f, fac_g, acc_ref):
    kb, taps = blocks.kb, blocks.taps
    for panel in range(blocks.panels):
        grad_z = None
        for i in range(blocks.kblocks):
            term = blocks.unmixed(g_ref[:, pl.ds(i * kb, kb)], panel, i)
            grad_z = term if grad_z is None else grad_z + term
        grad_f = (grad_z * fac_f[panel]).astype(jnp.bfloat16)
        grad_g = (grad_z * fac_g[panel]).astype(jnp.bfloat16)
        for i in range(blocks.kblocks):
            near = None
            for tap in range(taps):
                term = dot_t(grad_f, blocks.filt(tap, panel, i))
                term = term + dot_t(grad_g, blocks.gate(tap, panel, i))
                if tap < taps - 1:
                    term = up(term, shift)
                near = term if near is None else near + term
            add_to(acc_ref, pl.ds(i * kb, kb), near, panel == 0)


def flipped(values, index, count, block):
    shape = values.shape
    for bit in [1 << b for b in range(10) if 1 << b < count]:
        split = values.reshape(*shape[:-1], count // (2 * bit), 2, bit * block)
        values = jnp.where((index & bit) != 0, split[..., ::-1, :], split).reshape(shape)
    return values


def local(records, cotangent, filter_weight, gate_weight, mix_weight):
    layers = filter_weight.shape[0]
    rows, nb = records.shape
    kb = filter_weight.shape[2]
    tm_count, chan_count = lax.axis_size("tm"), lax.axis_size("chan")
    tm_index = lax.axis_index("tm")
    peers = tm_count * chan_count
    panels = chan_count // 2
    width = nb * chan_count
    bf16, f32 = jnp.bfloat16, jnp.float32
    square = kb == nb

    span = -(-rows // (4 * peers)) * 8
    padded = span * peers // 2
    m = tm_count * span

    taps_of = [2 if 2**layer < tm_count else 1 for layer in range(layers)]
    mix_source = mix_weight if square else mix_weight.transpose(0, 2, 1)
    sources = (filter_weight, gate_weight, mix_source)
    weights = Weights(packed(sources, taps_of), taps_of, HALVED, DEPTHS)

    def swap(values):
        return exchange(values, "chan", 1)

    both = jnp.pad(jnp.stack([records, cotangent]), ((0, 0), (0, padded - rows), (0, 0)))
    sent = both.reshape(2, peers // 2, span, nb).transpose(1, 0, 2, 3)
    sent = jnp.broadcast_to(sent[:, None], (peers // 2, 2, 2, span, nb)).reshape(peers, 2, span, nb)
    got = lax.all_to_all(sent, BOTH, split_axis=0, concat_axis=0, tiled=True)
    weights.begin([got])
    if not square:
        got = got.reshape(tm_count, chan_count, 2, span, nb).transpose(2, 0, 3, 1, 4)
        got = flipped(got.reshape(2, tm_count, span, width), tm_index, tm_count, kb)
        got = got.reshape(2, tm_count, span, tm_count, kb).transpose(1, 3, 0, 2, 4)
        got = got.reshape(tm_count * tm_count, 2, span, kb)

    def place(s, i):
        return s * tm_count + ((i ^ lax.axis_index("tm")) if square else i)

    def assemble(got_ref, which, target):
        for i in range(tm_count):
            parts = [got_ref[place(s, i), which].astype(f32) for s in range(tm_count)]
            target[:, pl.ds(i * kb, kb)] = jnp.concatenate(parts, axis=0).astype(bf16)

    vmem = pl.BlockSpec(memory_space=pltpu.VMEM)
    act = jax.ShapeDtypeStruct((m, width), bf16)
    fac = jax.ShapeDtypeStruct((panels, m, nb), f32)
    acc = [pltpu.VMEM((m, width), f32)]

    def layer_call(layer, body, arrays, held, outs, scratch, passes, name):
        taps, mats = taps_of[layer], 2 * taps_of[layer] + 1
        shift = 2**layer * span
        pieces = weights.layer(layer, arrays[1:2]) if held is None else []
        copies = sum(len(p.keys) for p in pieces)
        plan = [(p.keys, p.kind) for p in pieces]
        shape = (panels * tm_count, mats, kb, nb)
        elems = panels * tm_count * mats * kb * nb
        count = len(arrays)

        def kernel(*refs):
            ins, refs = refs[:count], refs[count:]
            if held is None:
                piece_refs, refs = refs[: len(pieces)], refs[len(pieces) :]
                blocks = Blocks(refs[len(outs)], panels, taps, square)
                blocks.fill(piece_refs, plan, refs[-1])
                body(blocks, shift, ins, refs[: len(outs)], refs[len(outs) + 1 : -1])
            else:
                blocks = Blocks(refs[0], panels, taps, square)
                body(blocks, shift, ins, refs[1 : 1 + len(outs)], refs[1 + len(outs) :])

        filling = held is None
        blocks_in = [p.array for p in pieces] if filling else [held]
        return pl.pallas_call(
            kernel,
            out_shape=[*outs, *([jax.ShapeDtypeStruct(shape, bf16)] if filling else [])],
            in_specs=[vmem] * count + [pl.BlockSpec(memory_space=pltpu.HBM if filling else pltpu.VMEM)] * len(blocks_in),
            out_specs=[vmem] * (len(outs) + filling),
            scratch_shapes=[*scratch, *([pltpu.SemaphoreType.DMA((copies,))] if filling else [])],
            compiler_params=pltpu.CompilerParams(vmem_limit_bytes=VMEM_LIMIT),
            cost_estimate=pl.CostEstimate(
                flops=2 * m * elems * passes, bytes_accessed=2 * elems, transcendentals=2 * m * nb
            ),
            name=name,
        )(*arrays, *blocks_in)

    def first_body(blocks, shift, ins, outs, scratch):
        sig, grad, part, fac_f, fac_g = outs
        assemble(ins[0], 0, sig)
        assemble(ins[0], 1, grad)
        forward_part(blocks, sig, shift, fac_f, fac_g, scratch[0])
        part[...] = scratch[0][...].astype(bf16)

    def forward_body(blocks, shift, ins, outs, scratch):
        sig, part, fac_f, fac_g = outs
        sig[...] = total(ins)
        forward_part(blocks, sig, shift, fac_f, fac_g, scratch[0])
        part[...] = scratch[0][...].astype(bf16)

    def last_body(blocks, shift, ins, outs, scratch):
        sig, part, gpart = outs
        fac_f, fac_g, acc_ref = scratch
        sig[...] = total(ins[:-1])
        forward_part(blocks, sig, shift, fac_f, fac_g, acc_ref)
        part[...] = acc_ref[...].astype(bf16)
        backward_part(blocks, ins[-1], shift, fac_f, fac_g, acc_ref)
        gpart[...] = acc_ref[...].astype(bf16)

    def backward_body(blocks, shift, ins, outs, scratch):
        now, part = outs
        now[...] = total(ins[:3])
        backward_part(blocks, now, shift, ins[3], ins[4], scratch[0])
        part[...] = scratch[0][...].astype(bf16)

    def final_body(blocks, shift, ins, outs, scratch):
        acc_ref, now = scratch
        now[...] = total(ins[:3])
        backward_part(blocks, now, shift, ins[3], ins[4], acc_ref)
        even = lax.axis_index("chan") % 2 == 0
        for i in range(tm_count):
            cols = pl.ds(i * kb, kb)
            base = now[:, cols].astype(f32)
            value = acc_ref[:, cols] + jnp.where(even, base, jnp.zeros_like(base))
            out = sum(ins[n][:, cols].astype(f32) for n in (6, 7)) + ins[5][:, cols].astype(f32)
            if square:
                out = jnp.where(even, out[:, : kb // 2], out[:, kb // 2 :])
            for s in range(tm_count):
                part = slice(s * span, (s + 1) * span)
                outs[0][place(s, i), :, :kb] = value[part].astype(bf16)
                outs[0][place(s, i), :, kb:] = out[part].astype(bf16)

    factors, helds = [], []
    sig, grad, part, fac_f, fac_g, held = layer_call(
        0, first_body, [got], None, [act, act, act, fac, fac], acc, 1, "layer_first"
    )
    for layer in range(1, layers - 1):
        factors.append((fac_f, fac_g))
        helds.append(held)
        sig, part, fac_f, fac_g, held = layer_call(
            layer, forward_body, [sig, part, swap(part)], None, [act, act, fac, fac], acc, 1, "layer_forward"
        )
    factors.append((fac_f, fac_g))
    helds.append(held)
    facs = [pltpu.VMEM((panels, m, nb), f32)] * 2
    sig, part, gpart, _ = layer_call(
        layers - 1,
        last_body,
        [sig, part, swap(part), grad],
        None,
        [act, act, act],
        facs + acc,
        2,
        "layer_last",
    )
    parts = [grad, gpart, swap(gpart)]
    output = [sig, part, swap(part)]
    for layer in reversed(range(1, layers - 1)):
        now, gpart = layer_call(
            layer,
            backward_body,
            [*parts, *factors[layer]],
            helds[layer],
            [act, act],
            acc,
            1,
            "layer_backward",
        )
        parts = [now, gpart, swap(gpart)]

    extra = kb // 2 if square else kb
    leaving = jax.ShapeDtypeStruct((tm_count * tm_count, span, kb + extra), bf16)
    back = layer_call(
        0,
        final_body,
        [*parts, *factors[0], *output],
        helds[0],
        [leaving],
        [*acc, pltpu.VMEM((m, width), bf16)],
        1,
        "layer_final",
    )[0]
    if not square:

        def regrouped(values):
            values = values.reshape(tm_count, tm_count, span, kb).transpose(0, 2, 1, 3)
            values = flipped(values.reshape(tm_count, span, width), tm_index, tm_count, kb)
            values = values.reshape(tm_count, span, chan_count, nb).transpose(0, 2, 1, 3)
            return values.reshape(peers, span, nb)

        out = regrouped(back[..., kb:])
        out = jnp.where(lax.axis_index("chan") % 2 == 0, out[..., : nb // 2], out[..., nb // 2 :])
        back = jnp.concatenate([regrouped(back[..., :kb]), out], axis=-1)
    back = lax.all_to_all(back, BOTH, split_axis=0, concat_axis=0, tiled=True)
    back = back.reshape(peers // 2, 2, span, nb + nb // 2)
    grads = back[..., :nb].astype(f32)
    input_grad = (grads[:, 0] + grads[:, 1]).astype(bf16).reshape(padded, nb)[:rows]
    output = jnp.concatenate([back[:, 0, :, nb:], back[:, 1, :, nb:]], axis=-1)
    return output.reshape(padded, nb)[:rows], input_grad


def solution(mesh):
    return jax.shard_map(
        local,
        mesh=mesh,
        in_specs=(
            P(("groups", "tm"), "chan"),
            P(("groups", "tm"), "chan"),
            P(None, None, "tm", "chan"),
            P(None, None, "tm", "chan"),
            P(None, "chan", "tm"),
        ),
        out_specs=(P(("groups", "tm"), "chan"), P(("groups", "tm"), "chan")),
        check_vma=False,
    )
```

```python
import jax
import jax.numpy as jnp
from jax import lax
from jax.experimental import pallas as pl
from jax.experimental.pallas import tpu as pltpu
from jax.sharding import PartitionSpec as P

BOTH = ("tm", "chan")
HALVED = ()
VMEM_LIMIT = 20 * 1024 * 1024


def dot(left, right):
    return jnp.dot(left, right, preferred_element_type=jnp.float32)


def dot_t(left, right):
    return lax.dot_general(
        left, right, (((1,), (1,)), ((), ())), preferred_element_type=jnp.float32
    )


def exchange(values, axis, bit):
    return lax.ppermute(values, axis, [(i, i ^ bit) for i in range(lax.axis_size(axis))])


def bits_of(axis, least):
    return [1 << b for b in range(10) if least <= 1 << b < lax.axis_size(axis)]


class Piece:
    def __init__(self, array, keys, kind):
        self.array, self.keys, self.kind = array, keys, kind

    def moved(self, axis, bit, kind=None):
        flip = {"chan": (bit, 0), "tm": (0, bit), "groups": (0, 0)}[axis]
        keys = [(k[0] ^ flip[0], k[1] ^ flip[1]) for k in self.keys]
        return Piece(exchange(self.array, axis, bit), keys, kind or self.kind)


def merged(pieces, limit):
    if len(pieces) <= limit:
        return pieces
    joined = []
    for kind in ("full", "mine", "other"):
        same = [p for p in pieces if p.kind == kind]
        if same:
            array = jnp.concatenate([p.array for p in same], axis=0)
            joined.append(Piece(array, sum((p.keys for p in same), []), kind))
    return joined


def packed(sources, taps_of, stages):
    kb, nb = sources[0].shape[2:]
    places, shapes = [], []
    for stage in stages:
        for rows in (kb // 2, kb):
            at = 0
            for layer in stage:
                places.append((len(shapes), layer, at))
                at += 2 * taps_of[layer] + 1
            shapes.append((1, at, rows, nb))

    def kernel(*refs):
        filt, gate, mix = refs[:3]
        outs, sems = refs[3:-1], refs[-1]
        copies = []
        for number, (n, layer, at) in enumerate(places):
            out, taps = outs[n], taps_of[layer]
            rows = out.shape[2]
            start = lax.axis_index("groups") * rows if n % 2 == 0 else 0
            window = pl.ds(pl.multiple_of(start, rows), rows)
            for w, ref in enumerate((filt, gate)):
                source = ref.at[layer, pl.ds(2 - taps, taps), window]
                target = out.at[0, pl.ds(at + w * taps, taps)]
                copies.append(pltpu.make_async_copy(source, target, sems.at[number, w]))
            target = out.at[0, at + 2 * taps]
            copies.append(pltpu.make_async_copy(mix.at[layer, window], target, sems.at[number, 2]))
        for copy in copies:
            copy.start()
        for copy in copies:
            copy.wait()

    return pl.pallas_call(
        kernel,
        out_shape=[jax.ShapeDtypeStruct(shape, jnp.bfloat16) for shape in shapes],
        in_specs=[pl.BlockSpec(memory_space=pl.ANY)] * 3,
        out_specs=[pl.BlockSpec(memory_space=pltpu.VMEM)] * len(shapes),
        scratch_shapes=[pltpu.SemaphoreType.DMA((len(places), 3))],
        name="pack",
    )(*sources)


def ordered(piece, axis, bit, kind=None, after=()):
    if after:
        piece.array = lax.optimization_barrier((piece.array, *after))[0]
    return piece.moved(axis, bit, kind)


class Weights:
    def __init__(self, packs, halved):
        self.limit = 16 if lax.axis_size("tm") <= 4 and lax.axis_size("chan") <= 4 else 1
        self.halved, self.high = halved, bits_of("tm", 2)
        count = len(packs) // 2
        self.halves = [Piece(packs[2 * n], [(0, 0)], "mine") for n in range(count)]
        self.full = [[Piece(packs[2 * n + 1], [(0, 0)], "full")] for n in range(count)]
        self.zs, self.ys, self.crossed, self.others = ([[] for _ in range(count)] for _ in range(4))

    def along_chan(self, n, after=()):
        for bit in bits_of("chan", 2):
            sources = [self.halves[n]] + self.zs[n]
            self.zs[n] = self.zs[n] + [ordered(p, "chan", bit, None, after) for p in sources]

    def own_along_tm(self, n, after=()):
        for bit in self.high:
            if n in self.halved:
                sources = [self.halves[n]] + self.ys[n]
                self.ys[n] = self.ys[n] + [ordered(p, "tm", bit, None, after) for p in sources]
            else:
                moved = [ordered(p, "tm", bit, None, after) for p in self.full[n]]
                self.full[n] = self.full[n] + moved

    def others_along_tm(self, n, after=()):
        for bit in self.high:
            sources = merged(self.zs[n] + self.crossed[n], self.limit)
            self.crossed[n] = self.crossed[n] + [
                ordered(p, "tm", bit, None, after) for p in sources
            ]

    def along_groups(self, n, pieces, after=()):
        for p in merged(pieces, self.limit):
            self.others[n].append(ordered(p, "groups", 1, "other", after))

    def send(self, exchange_rows):
        def arrays(*lists):
            return [p.array for pieces in lists for p in pieces]

        self.along_chan(0)
        self.own_along_tm(0)
        ended = arrays(self.zs[0], self.ys[0], self.full[0][1:])
        self.others_along_tm(0, ended)
        self.along_groups(0, self.zs[0] + self.ys[0], ended)
        self.along_chan(1, ended)
        ended = arrays(self.crossed[0], self.others[0], self.zs[1])
        rows = exchange_rows(ended)
        self.along_groups(0, self.crossed[0], ended)
        self.others_along_tm(1, ended)
        ended = arrays(self.others[0])
        self.along_groups(1, self.zs[1], ended)
        self.own_along_tm(1, ended)
        ended = arrays(self.crossed[1])
        rows = lax.optimization_barrier((rows, *ended))[0]
        return rows, self.stage(0)

    def own_halves(self, after):
        self.along_groups(1, self.ys[1], after)

    def middle(self):
        return [p.array for p in self.ys[1] + self.full[1][1:] + self.others[1]]

    def finish(self, before, after):
        first = [p.array for p in self.ys[1] + self.full[1][1:] + self.others[1]]
        self.along_groups(1, self.crossed[1], [*before, *first])
        return self.stage(1, after)

    def stage(self, n, after=()):
        pieces = self.full[n] + self.ys[n] + self.zs[n] + self.crossed[n] + self.others[n]
        pieces = merged(pieces, self.limit)
        if lax.axis_size("tm") > 1:
            pieces = pieces + [ordered(p, "tm", 1, None, after) for p in pieces]
        return pieces


class Blocks:
    def __init__(self, held, panels, taps, square):
        self.held, self.panels, self.taps, self.square = held, panels, taps, square
        self.kblocks = held.shape[0] // panels
        self.kb = held.shape[2]
        self.copies = {}

    def fill(self, refs, plan, at, sems):
        group = lax.axis_index("groups")
        half = self.kb // 2
        number = 0
        for ref, (keys, kind) in zip(refs, plan):
            for lead, (dz, dtm) in enumerate(keys):
                target = self.held.at[dz // 2 * self.kblocks + dtm]
                if kind != "full":
                    which = group if kind == "mine" else 1 - group
                    window = pl.ds(pl.multiple_of(which * half, half), half)
                    target = self.held.at[dz // 2 * self.kblocks + dtm, :, window]
                mats = pl.ds(at, self.held.shape[1])
                copy = pltpu.make_async_copy(ref.at[lead, mats], target, sems.at[number])
                self.copies.setdefault((dz // 2, dtm), []).append(copy)
                number += 1
        for panel in range(self.panels):
            for i in range(self.kblocks):
                for copy in self.copies[panel, i]:
                    copy.start()

    def wait(self, panel, i):
        for copy in self.copies.pop((panel, i), []):
            copy.wait()

    def mat(self, which, panel, i):
        return self.held[panel * self.kblocks + i, which]

    def filt(self, tap, panel, i):
        return self.mat(tap, panel, i)

    def gate(self, tap, panel, i):
        return self.mat(self.taps + tap, panel, i)

    def mixed(self, gated, panel, i):
        mix = self.mat(2 * self.taps, panel, i)
        return dot(gated, mix) if self.square else dot_t(gated, mix)

    def unmixed(self, grad, panel, i):
        mix = self.mat(2 * self.taps, panel, i)
        return dot_t(grad, mix) if self.square else dot(grad, mix)


def down(values, rows):
    return jnp.concatenate([jnp.zeros_like(values[:rows]), values[: values.shape[0] - rows]], axis=0)


def up(values, rows):
    return jnp.concatenate([values[rows:], jnp.zeros_like(values[:rows])], axis=0)


def total(parts):
    if len(parts) == 1:
        return parts[0][...]
    base, own, other = (part[...].astype(jnp.float32) for part in parts)
    return (base + (own + other)).astype(jnp.bfloat16)


def add_to(acc_ref, cols, term, first):
    if first:
        acc_ref[:, cols] = term
    else:
        acc_ref[:, cols] += term


def forward_part(blocks, x_ref, shift, fac_f, fac_g, acc_ref):
    kb, taps = blocks.kb, blocks.taps
    for panel in range(blocks.panels):
        sums = [[None] * taps, [None] * taps]
        for i in range(blocks.kblocks):
            blocks.wait(panel, i)
            x = x_ref[:, pl.ds(i * kb, kb)]
            for n, kernel in enumerate((blocks.filt, blocks.gate)):
                for tap in range(taps):
                    term = dot(x, kernel(tap, panel, i))
                    sums[n][tap] = term if i == 0 else sums[n][tap] + term
        pre = [s[-1] if taps == 1 else s[-1] + down(s[0], shift) for s in sums]
        tanh_value = jnp.tanh(pre[0])
        sig_value = jax.nn.sigmoid(pre[1])
        gated = (tanh_value * sig_value).astype(jnp.bfloat16)
        fac_f[panel] = sig_value * (1.0 - tanh_value * tanh_value)
        fac_g[panel] = tanh_value * sig_value * (1.0 - sig_value)
        for i in range(blocks.kblocks):
            add_to(acc_ref, pl.ds(i * kb, kb), blocks.mixed(gated, panel, i), panel == 0)


def backward_part(blocks, g_ref, shift, fac_f, fac_g, acc_ref):
    kb, taps = blocks.kb, blocks.taps
    for panel in range(blocks.panels):
        grad_z = None
        for i in range(blocks.kblocks):
            term = blocks.unmixed(g_ref[:, pl.ds(i * kb, kb)], panel, i)
            grad_z = term if grad_z is None else grad_z + term
        grad_f = (grad_z * fac_f[panel]).astype(jnp.bfloat16)
        grad_g = (grad_z * fac_g[panel]).astype(jnp.bfloat16)
        for i in range(blocks.kblocks):
            near = None
            for tap in range(taps):
                term = dot_t(grad_f, blocks.filt(tap, panel, i))
                term = term + dot_t(grad_g, blocks.gate(tap, panel, i))
                if tap < taps - 1:
                    term = up(term, shift)
                near = term if near is None else near + term
            add_to(acc_ref, pl.ds(i * kb, kb), near, panel == 0)


def flipped(values, index, count, block):
    shape = values.shape
    for bit in [1 << b for b in range(10) if 1 << b < count]:
        split = values.reshape(*shape[:-1], count // (2 * bit), 2, bit * block)
        values = jnp.where((index & bit) != 0, split[..., ::-1, :], split).reshape(shape)
    return values


def local(records, cotangent, filter_weight, gate_weight, mix_weight):
    layers = filter_weight.shape[0]
    rows, nb = records.shape
    kb = filter_weight.shape[2]
    tm_count, chan_count = lax.axis_size("tm"), lax.axis_size("chan")
    tm_index = lax.axis_index("tm")
    peers = tm_count * chan_count
    panels = chan_count // 2
    width = nb * chan_count
    bf16, f32 = jnp.bfloat16, jnp.float32
    square = kb == nb

    span = -(-rows // (4 * peers)) * 8
    padded = span * peers // 2
    m = tm_count * span

    taps_of = [2 if 2**layer < tm_count else 1 for layer in range(layers)]
    mix_source = mix_weight if square else mix_weight.transpose(0, 2, 1)
    sources = (filter_weight, gate_weight, mix_source)
    early = (layers + 1) // 2
    stages = [range(early), range(early, layers)]
    weights = Weights(packed(sources, taps_of, stages), HALVED)

    def swap(values):
        return exchange(values, "chan", 1)

    both = jnp.pad(jnp.stack([records, cotangent]), ((0, 0), (0, padded - rows), (0, 0)))
    sent = both.reshape(2, peers // 2, span, nb).transpose(1, 0, 2, 3)
    sent = jnp.broadcast_to(sent[:, None], (peers // 2, 2, 2, span, nb)).reshape(peers, 2, span, nb)

    def exchange_rows(after):
        ready = lax.optimization_barrier((sent, *after))[0]
        return lax.all_to_all(ready, BOTH, split_axis=0, concat_axis=0, tiled=True)

    got, pieces = weights.send(exchange_rows)
    pieces_of = [pieces]
    if not square:
        got = got.reshape(tm_count, chan_count, 2, span, nb).transpose(2, 0, 3, 1, 4)
        got = flipped(got.reshape(2, tm_count, span, width), tm_index, tm_count, kb)
        got = got.reshape(2, tm_count, span, tm_count, kb).transpose(1, 3, 0, 2, 4)
        got = got.reshape(tm_count * tm_count, 2, span, kb)

    def place(s, i):
        return s * tm_count + ((i ^ lax.axis_index("tm")) if square else i)

    def assemble(got_ref, which, target):
        for i in range(tm_count):
            parts = [got_ref[place(s, i), which].astype(f32) for s in range(tm_count)]
            target[:, pl.ds(i * kb, kb)] = jnp.concatenate(parts, axis=0).astype(bf16)

    vmem = pl.BlockSpec(memory_space=pltpu.VMEM)
    act = jax.ShapeDtypeStruct((m, width), bf16)
    fac = jax.ShapeDtypeStruct((panels, m, nb), f32)
    acc = [pltpu.VMEM((m, width), f32)]

    def layer_call(layer, body, arrays, held, outs, scratch, passes, name):
        taps, mats = taps_of[layer], 2 * taps_of[layer] + 1
        shift = 2**layer * span
        pieces = pieces_of[layer // early] if held is None else []
        at = sum(2 * taps_of[n] + 1 for n in range(layer // early * early, layer))
        copies = sum(len(p.keys) for p in pieces)
        plan = [(p.keys, p.kind) for p in pieces]
        shape = (panels * tm_count, mats, kb, nb)
        elems = panels * tm_count * mats * kb * nb
        count = len(arrays)

        def kernel(*refs):
            ins, refs = refs[:count], refs[count:]
            if held is None:
                piece_refs, refs = refs[: len(pieces)], refs[len(pieces) :]
                blocks = Blocks(refs[len(outs)], panels, taps, square)
                blocks.fill(piece_refs, plan, at, refs[-1])
                body(blocks, shift, ins, refs[: len(outs)], refs[len(outs) + 1 : -1])
            else:
                blocks = Blocks(refs[0], panels, taps, square)
                body(blocks, shift, ins, refs[1 : 1 + len(outs)], refs[1 + len(outs) :])

        filling = held is None
        blocks_in = [p.array for p in pieces] if filling else [held]
        return pl.pallas_call(
            kernel,
            out_shape=[*outs, *([jax.ShapeDtypeStruct(shape, bf16)] if filling else [])],
            in_specs=[vmem] * count + [pl.BlockSpec(memory_space=pl.ANY if filling else pltpu.VMEM)] * len(blocks_in),
            out_specs=[vmem] * (len(outs) + filling),
            scratch_shapes=[*scratch, *([pltpu.SemaphoreType.DMA((copies,))] if filling else [])],
            compiler_params=pltpu.CompilerParams(vmem_limit_bytes=VMEM_LIMIT),
            cost_estimate=pl.CostEstimate(
                flops=2 * m * elems * passes, bytes_accessed=2 * elems, transcendentals=2 * m * nb
            ),
            name=name,
        )(*arrays, *blocks_in)

    def first_body(blocks, shift, ins, outs, scratch):
        sig, grad, part, fac_f, fac_g = outs
        assemble(ins[0], 0, sig)
        assemble(ins[0], 1, grad)
        forward_part(blocks, sig, shift, fac_f, fac_g, scratch[0])
        part[...] = scratch[0][...].astype(bf16)

    def forward_body(blocks, shift, ins, outs, scratch):
        sig, part, fac_f, fac_g = outs
        sig[...] = total(ins)
        forward_part(blocks, sig, shift, fac_f, fac_g, scratch[0])
        part[...] = scratch[0][...].astype(bf16)

    def last_body(blocks, shift, ins, outs, scratch):
        sig, part, gpart = outs
        fac_f, fac_g, acc_ref = scratch
        sig[...] = total(ins[:-1])
        forward_part(blocks, sig, shift, fac_f, fac_g, acc_ref)
        part[...] = acc_ref[...].astype(bf16)
        backward_part(blocks, ins[-1], shift, fac_f, fac_g, acc_ref)
        gpart[...] = acc_ref[...].astype(bf16)

    def backward_body(blocks, shift, ins, outs, scratch):
        now, part = outs
        now[...] = total(ins[:3])
        backward_part(blocks, now, shift, ins[3], ins[4], scratch[0])
        part[...] = scratch[0][...].astype(bf16)

    def final_body(blocks, shift, ins, outs, scratch):
        acc_ref, now = scratch
        now[...] = total(ins[:3])
        backward_part(blocks, now, shift, ins[3], ins[4], acc_ref)
        even = lax.axis_index("chan") % 2 == 0
        for i in range(tm_count):
            cols = pl.ds(i * kb, kb)
            base = now[:, cols].astype(f32)
            value = acc_ref[:, cols] + jnp.where(even, base, jnp.zeros_like(base))
            out = sum(ins[n][:, cols].astype(f32) for n in (6, 7)) + ins[5][:, cols].astype(f32)
            if square:
                out = jnp.where(even, out[:, : kb // 2], out[:, kb // 2 :])
            for s in range(tm_count):
                part = slice(s * span, (s + 1) * span)
                outs[0][place(s, i), :, :kb] = value[part].astype(bf16)
                outs[0][place(s, i), :, kb:] = out[part].astype(bf16)

    factors, helds = [], []
    sig, grad, part, fac_f, fac_g, held = layer_call(
        0, first_body, [got], None, [act, act, act, fac, fac], acc, 1, "layer_first"
    )
    weights.own_halves([part])
    for layer in range(1, layers - 1):
        arrived = swap(part)
        if layer == 1:
            arrived = lax.optimization_barrier((arrived, *weights.middle()))[0]
        if layer == early:
            pieces_of.append(weights.finish([part], [arrived]))
        factors.append((fac_f, fac_g))
        helds.append(held)
        sig, part, fac_f, fac_g, held = layer_call(
            layer, forward_body, [sig, part, arrived], None, [act, act, fac, fac], acc, 1, "layer_forward"
        )
    factors.append((fac_f, fac_g))
    helds.append(held)
    facs = [pltpu.VMEM((panels, m, nb), f32)] * 2
    sig, part, gpart, _ = layer_call(
        layers - 1,
        last_body,
        [sig, part, swap(part), grad],
        None,
        [act, act, act],
        facs + acc,
        2,
        "layer_last",
    )
    parts = [grad, gpart, swap(gpart)]
    output = [sig, part, swap(part)]
    for layer in reversed(range(1, layers - 1)):
        now, gpart = layer_call(
            layer,
            backward_body,
            [*parts, *factors[layer]],
            helds[layer],
            [act, act],
            acc,
            1,
            "layer_backward",
        )
        parts = [now, gpart, swap(gpart)]

    extra = kb // 2 if square else kb
    leaving = jax.ShapeDtypeStruct((tm_count * tm_count, span, kb + extra), bf16)
    back = layer_call(
        0,
        final_body,
        [*parts, *factors[0], *output],
        helds[0],
        [leaving],
        [*acc, pltpu.VMEM((m, width), bf16)],
        1,
        "layer_final",
    )[0]
    if not square:

        def regrouped(values):
            values = values.reshape(tm_count, tm_count, span, kb).transpose(0, 2, 1, 3)
            values = flipped(values.reshape(tm_count, span, width), tm_index, tm_count, kb)
            values = values.reshape(tm_count, span, chan_count, nb).transpose(0, 2, 1, 3)
            return values.reshape(peers, span, nb)

        out = regrouped(back[..., kb:])
        out = jnp.where(lax.axis_index("chan") % 2 == 0, out[..., : nb // 2], out[..., nb // 2 :])
        back = jnp.concatenate([regrouped(back[..., :kb]), out], axis=-1)
    back = lax.all_to_all(back, BOTH, split_axis=0, concat_axis=0, tiled=True)
    back = back.reshape(peers // 2, 2, span, nb + nb // 2)
    grads = back[..., :nb].astype(f32)
    input_grad = (grads[:, 0] + grads[:, 1]).astype(bf16).reshape(padded, nb)[:rows]
    output = jnp.concatenate([back[:, 0, :, nb:], back[:, 1, :, nb:]], axis=-1)
    return output.reshape(padded, nb)[:rows], input_grad


def solution(mesh):
    return jax.shard_map(
        local,
        mesh=mesh,
        in_specs=(
            P(("groups", "tm"), "chan"),
            P(("groups", "tm"), "chan"),
            P(None, None, "tm", "chan"),
            P(None, None, "tm", "chan"),
            P(None, "chan", "tm"),
        ),
        out_specs=(P(("groups", "tm"), "chan"), P(("groups", "tm"), "chan")),
        check_vma=False,
    )
```

```python
import jax
import jax.numpy as jnp
from jax import lax
from jax.experimental import pallas as pl
from jax.experimental.pallas import tpu as pltpu
from jax.sharding import PartitionSpec as P

BOTH = ("tm", "chan")
HALVED = ()
VMEM_LIMIT = 20 * 1024 * 1024


def dot(left, right):
    return jnp.dot(left, right, preferred_element_type=jnp.float32)


def dot_t(left, right):
    return lax.dot_general(
        left, right, (((1,), (1,)), ((), ())), preferred_element_type=jnp.float32
    )


def exchange(values, axis, bit):
    return lax.ppermute(values, axis, [(i, i ^ bit) for i in range(lax.axis_size(axis))])


def bits_of(axis, least):
    return [1 << b for b in range(10) if least <= 1 << b < lax.axis_size(axis)]


class Piece:
    def __init__(self, array, keys, kind):
        self.array, self.keys, self.kind = array, keys, kind

    def moved(self, axis, bit, kind=None):
        flip = {"chan": (bit, 0), "tm": (0, bit), "groups": (0, 0)}[axis]
        keys = [(k[0] ^ flip[0], k[1] ^ flip[1]) for k in self.keys]
        return Piece(exchange(self.array, axis, bit), keys, kind or self.kind)


def merged(pieces, limit):
    if len(pieces) <= limit:
        return pieces
    joined = []
    for kind in ("full", "mine", "other"):
        same = [p for p in pieces if p.kind == kind]
        if same:
            array = jnp.concatenate([p.array for p in same], axis=0)
            joined.append(Piece(array, sum((p.keys for p in same), []), kind))
    return joined


def packed(sources, taps_of, stages):
    kb, nb = sources[0].shape[2:]
    places, shapes = [], []
    for stage in stages:
        for rows in (kb // 2, kb):
            at = 0
            for layer in stage:
                places.append((len(shapes), layer, at))
                at += 2 * taps_of[layer] + 1
            shapes.append((1, at, rows, nb))

    def kernel(*refs):
        filt, gate, mix = refs[:3]
        outs, sems = refs[3:-1], refs[-1]
        copies = []
        for number, (n, layer, at) in enumerate(places):
            out, taps = outs[n], taps_of[layer]
            rows = out.shape[2]
            start = lax.axis_index("groups") * rows if n % 2 == 0 else 0
            window = pl.ds(pl.multiple_of(start, rows), rows)
            for w, ref in enumerate((filt, gate)):
                source = ref.at[layer, pl.ds(2 - taps, taps), window]
                target = out.at[0, pl.ds(at + w * taps, taps)]
                copies.append(pltpu.make_async_copy(source, target, sems.at[number, w]))
            target = out.at[0, at + 2 * taps]
            copies.append(pltpu.make_async_copy(mix.at[layer, window], target, sems.at[number, 2]))
        for copy in copies:
            copy.start()
        for copy in copies:
            copy.wait()

    return pl.pallas_call(
        kernel,
        out_shape=[jax.ShapeDtypeStruct(shape, jnp.bfloat16) for shape in shapes],
        in_specs=[pl.BlockSpec(memory_space=pl.ANY)] * 3,
        out_specs=[pl.BlockSpec(memory_space=pltpu.VMEM)] * len(shapes),
        scratch_shapes=[pltpu.SemaphoreType.DMA((len(places), 3))],
        name="pack",
    )(*sources)


def ordered(piece, axis, bit, kind=None, after=()):
    if after:
        piece.array = lax.optimization_barrier((piece.array, *after))[0]
    return piece.moved(axis, bit, kind)


class Weights:
    def __init__(self, packs, halved):
        self.limit = 16 if lax.axis_size("tm") <= 4 and lax.axis_size("chan") <= 4 else 1
        self.halved, self.high = halved, bits_of("tm", 2)
        count = len(packs) // 2
        self.halves = [Piece(packs[2 * n], [(0, 0)], "mine") for n in range(count)]
        self.full = [[Piece(packs[2 * n + 1], [(0, 0)], "full")] for n in range(count)]
        self.zs, self.ys, self.crossed, self.others = ([[] for _ in range(count)] for _ in range(4))

    def along_chan(self, n, after=()):
        for bit in bits_of("chan", 2):
            sources = [self.halves[n]] + self.zs[n]
            self.zs[n] = self.zs[n] + [ordered(p, "chan", bit, None, after) for p in sources]

    def own_along_tm(self, n, after=()):
        for bit in self.high:
            if n in self.halved:
                sources = [self.halves[n]] + self.ys[n]
                self.ys[n] = self.ys[n] + [ordered(p, "tm", bit, None, after) for p in sources]
            else:
                moved = [ordered(p, "tm", bit, None, after) for p in self.full[n]]
                self.full[n] = self.full[n] + moved

    def others_along_tm(self, n, after=()):
        for bit in self.high:
            sources = merged(self.zs[n] + self.crossed[n], self.limit)
            self.crossed[n] = self.crossed[n] + [
                ordered(p, "tm", bit, None, after) for p in sources
            ]

    def along_groups(self, n, pieces, after=()):
        for p in merged(pieces, self.limit):
            self.others[n].append(ordered(p, "groups", 1, "other", after))

    def send(self, exchange_rows, sent):
        def arrays(*lists):
            return [p.array for pieces in lists for p in pieces]

        self.along_chan(0)
        self.own_along_tm(0)
        ended = arrays(self.zs[0], self.ys[0], self.full[0][1:], [self.halves[1]], self.full[1])
        ended.append(sent)
        self.others_along_tm(0, ended)
        self.along_groups(0, self.zs[0] + self.ys[0], ended)
        self.along_chan(1, ended)
        ended = arrays(self.crossed[0], self.others[0], self.zs[1])
        rows = exchange_rows(ended)
        self.along_groups(0, self.crossed[0], ended)
        self.others_along_tm(1, ended)
        ended = arrays(self.others[0])
        self.along_groups(1, self.zs[1], ended)
        self.own_along_tm(1, ended)
        ended = arrays(self.crossed[1])
        rows = lax.optimization_barrier((rows, *ended))[0]
        return rows, self.stage(0)

    def own_halves(self, after):
        self.along_groups(1, self.ys[1], after)

    def middle(self):
        return [p.array for p in self.ys[1] + self.full[1][1:] + self.others[1]]

    def finish(self, before, after):
        self.along_groups(1, self.crossed[1], before)
        return self.stage(1, after)

    def stage(self, n, after=()):
        pieces = self.full[n] + self.ys[n] + self.zs[n] + self.crossed[n] + self.others[n]
        pieces = merged(pieces, self.limit)
        if lax.axis_size("tm") > 1:
            pieces = pieces + [ordered(p, "tm", 1, None, after) for p in pieces]
        return pieces


class Blocks:
    def __init__(self, held, panels, taps, square):
        self.held, self.panels, self.taps, self.square = held, panels, taps, square
        self.kblocks = held.shape[0] // panels
        self.kb = held.shape[2]
        self.copies = {}

    def fill(self, refs, plan, at, sems):
        group = lax.axis_index("groups")
        half = self.kb // 2
        number = 0
        for ref, (keys, kind) in zip(refs, plan):
            for lead, (dz, dtm) in enumerate(keys):
                target = self.held.at[dz // 2 * self.kblocks + dtm]
                if kind != "full":
                    which = group if kind == "mine" else 1 - group
                    window = pl.ds(pl.multiple_of(which * half, half), half)
                    target = self.held.at[dz // 2 * self.kblocks + dtm, :, window]
                mats = pl.ds(at, self.held.shape[1])
                copy = pltpu.make_async_copy(ref.at[lead, mats], target, sems.at[number])
                self.copies.setdefault((dz // 2, dtm), []).append(copy)
                number += 1
        for panel in range(self.panels):
            for i in range(self.kblocks):
                for copy in self.copies[panel, i]:
                    copy.start()

    def wait(self, panel, i):
        for copy in self.copies.pop((panel, i), []):
            copy.wait()

    def mat(self, which, panel, i):
        return self.held[panel * self.kblocks + i, which]

    def filt(self, tap, panel, i):
        return self.mat(tap, panel, i)

    def gate(self, tap, panel, i):
        return self.mat(self.taps + tap, panel, i)

    def mixed(self, gated, panel, i):
        mix = self.mat(2 * self.taps, panel, i)
        return dot(gated, mix) if self.square else dot_t(gated, mix)

    def unmixed(self, grad, panel, i):
        mix = self.mat(2 * self.taps, panel, i)
        return dot_t(grad, mix) if self.square else dot(grad, mix)


def down(values, rows):
    return jnp.concatenate([jnp.zeros_like(values[:rows]), values[: values.shape[0] - rows]], axis=0)


def up(values, rows):
    return jnp.concatenate([values[rows:], jnp.zeros_like(values[:rows])], axis=0)


def total(parts):
    if len(parts) == 1:
        return parts[0][...]
    base, own, other = (part[...].astype(jnp.float32) for part in parts)
    return (base + (own + other)).astype(jnp.bfloat16)


def add_to(acc_ref, cols, term, first):
    if first:
        acc_ref[:, cols] = term
    else:
        acc_ref[:, cols] += term


def forward_part(blocks, x_ref, shift, fac_f, fac_g, acc_ref):
    kb, taps = blocks.kb, blocks.taps
    for panel in range(blocks.panels):
        sums = [[None] * taps, [None] * taps]
        for i in range(blocks.kblocks):
            blocks.wait(panel, i)
            x = x_ref[:, pl.ds(i * kb, kb)]
            for n, kernel in enumerate((blocks.filt, blocks.gate)):
                for tap in range(taps):
                    term = dot(x, kernel(tap, panel, i))
                    sums[n][tap] = term if i == 0 else sums[n][tap] + term
        pre = [s[-1] if taps == 1 else s[-1] + down(s[0], shift) for s in sums]
        tanh_value = jnp.tanh(pre[0])
        sig_value = jax.nn.sigmoid(pre[1])
        gated = (tanh_value * sig_value).astype(jnp.bfloat16)
        fac_f[panel] = sig_value * (1.0 - tanh_value * tanh_value)
        fac_g[panel] = tanh_value * sig_value * (1.0 - sig_value)
        for i in range(blocks.kblocks):
            add_to(acc_ref, pl.ds(i * kb, kb), blocks.mixed(gated, panel, i), panel == 0)


def backward_part(blocks, g_ref, shift, fac_f, fac_g, acc_ref):
    kb, taps = blocks.kb, blocks.taps
    for panel in range(blocks.panels):
        grad_z = None
        for i in range(blocks.kblocks):
            term = blocks.unmixed(g_ref[:, pl.ds(i * kb, kb)], panel, i)
            grad_z = term if grad_z is None else grad_z + term
        grad_f = (grad_z * fac_f[panel]).astype(jnp.bfloat16)
        grad_g = (grad_z * fac_g[panel]).astype(jnp.bfloat16)
        for i in range(blocks.kblocks):
            near = None
            for tap in range(taps):
                term = dot_t(grad_f, blocks.filt(tap, panel, i))
                term = term + dot_t(grad_g, blocks.gate(tap, panel, i))
                if tap < taps - 1:
                    term = up(term, shift)
                near = term if near is None else near + term
            add_to(acc_ref, pl.ds(i * kb, kb), near, panel == 0)


def flipped(values, index, count, block):
    shape = values.shape
    for bit in [1 << b for b in range(10) if 1 << b < count]:
        split = values.reshape(*shape[:-1], count // (2 * bit), 2, bit * block)
        values = jnp.where((index & bit) != 0, split[..., ::-1, :], split).reshape(shape)
    return values


def local(records, cotangent, filter_weight, gate_weight, mix_weight):
    layers = filter_weight.shape[0]
    rows, nb = records.shape
    kb = filter_weight.shape[2]
    tm_count, chan_count = lax.axis_size("tm"), lax.axis_size("chan")
    tm_index = lax.axis_index("tm")
    peers = tm_count * chan_count
    panels = chan_count // 2
    width = nb * chan_count
    bf16, f32 = jnp.bfloat16, jnp.float32
    square = kb == nb

    span = -(-rows // (4 * peers)) * 8
    padded = span * peers // 2
    m = tm_count * span

    taps_of = [2 if 2**layer < tm_count else 1 for layer in range(layers)]
    mix_source = mix_weight if square else mix_weight.transpose(0, 2, 1)
    sources = (filter_weight, gate_weight, mix_source)
    early = (layers + 1) // 2
    stages = [range(early), range(early, layers)]
    packs = [array for stage in stages for array in packed(sources, taps_of, [stage])]
    weights = Weights(packs, HALVED)

    def swap(values):
        return exchange(values, "chan", 1)

    both = jnp.pad(jnp.stack([records, cotangent]), ((0, 0), (0, padded - rows), (0, 0)))
    sent = both.reshape(2, peers // 2, span, nb).transpose(1, 0, 2, 3)
    sent = jnp.broadcast_to(sent[:, None], (peers // 2, 2, 2, span, nb)).reshape(peers, 2, span, nb)

    def exchange_rows(after):
        ready = lax.optimization_barrier((sent, *after))[0]
        return lax.all_to_all(ready, BOTH, split_axis=0, concat_axis=0, tiled=True)

    got, pieces = weights.send(exchange_rows, sent)
    pieces_of = [pieces]
    if not square:
        got = got.reshape(tm_count, chan_count, 2, span, nb).transpose(2, 0, 3, 1, 4)
        got = flipped(got.reshape(2, tm_count, span, width), tm_index, tm_count, kb)
        got = got.reshape(2, tm_count, span, tm_count, kb).transpose(1, 3, 0, 2, 4)
        got = got.reshape(tm_count * tm_count, 2, span, kb)

    def place(s, i):
        return s * tm_count + ((i ^ lax.axis_index("tm")) if square else i)

    def assemble(got_ref, which, target):
        for i in range(tm_count):
            parts = [got_ref[place(s, i), which].astype(f32) for s in range(tm_count)]
            target[:, pl.ds(i * kb, kb)] = jnp.concatenate(parts, axis=0).astype(bf16)

    vmem = pl.BlockSpec(memory_space=pltpu.VMEM)
    act = jax.ShapeDtypeStruct((m, width), bf16)
    fac = jax.ShapeDtypeStruct((panels, m, nb), f32)
    acc = [pltpu.VMEM((m, width), f32)]

    def layer_call(layer, body, arrays, held, outs, scratch, passes, name):
        taps, mats = taps_of[layer], 2 * taps_of[layer] + 1
        shift = 2**layer * span
        pieces = pieces_of[layer // early] if held is None else []
        at = sum(2 * taps_of[n] + 1 for n in range(layer // early * early, layer))
        copies = sum(len(p.keys) for p in pieces)
        plan = [(p.keys, p.kind) for p in pieces]
        shape = (panels * tm_count, mats, kb, nb)
        elems = panels * tm_count * mats * kb * nb
        count = len(arrays)

        def kernel(*refs):
            ins, refs = refs[:count], refs[count:]
            if held is None:
                piece_refs, refs = refs[: len(pieces)], refs[len(pieces) :]
                blocks = Blocks(refs[len(outs)], panels, taps, square)
                blocks.fill(piece_refs, plan, at, refs[-1])
                body(blocks, shift, ins, refs[: len(outs)], refs[len(outs) + 1 : -1])
            else:
                blocks = Blocks(refs[0], panels, taps, square)
                body(blocks, shift, ins, refs[1 : 1 + len(outs)], refs[1 + len(outs) :])

        filling = held is None
        blocks_in = [p.array for p in pieces] if filling else [held]
        return pl.pallas_call(
            kernel,
            out_shape=[*outs, *([jax.ShapeDtypeStruct(shape, bf16)] if filling else [])],
            in_specs=[vmem] * count + [pl.BlockSpec(memory_space=pl.ANY if filling else pltpu.VMEM)] * len(blocks_in),
            out_specs=[vmem] * (len(outs) + filling),
            scratch_shapes=[*scratch, *([pltpu.SemaphoreType.DMA((copies,))] if filling else [])],
            compiler_params=pltpu.CompilerParams(vmem_limit_bytes=VMEM_LIMIT),
            cost_estimate=pl.CostEstimate(
                flops=2 * m * elems * passes, bytes_accessed=2 * elems, transcendentals=2 * m * nb
            ),
            name=name,
        )(*arrays, *blocks_in)

    def first_body(blocks, shift, ins, outs, scratch):
        sig, grad, part, fac_f, fac_g = outs
        assemble(ins[0], 0, sig)
        assemble(ins[0], 1, grad)
        forward_part(blocks, sig, shift, fac_f, fac_g, scratch[0])
        part[...] = scratch[0][...].astype(bf16)

    def forward_body(blocks, shift, ins, outs, scratch):
        sig, part, fac_f, fac_g = outs
        sig[...] = total(ins)
        forward_part(blocks, sig, shift, fac_f, fac_g, scratch[0])
        part[...] = scratch[0][...].astype(bf16)

    def last_body(blocks, shift, ins, outs, scratch):
        sig, part, gpart = outs
        fac_f, fac_g, acc_ref = scratch
        sig[...] = total(ins[:-1])
        forward_part(blocks, sig, shift, fac_f, fac_g, acc_ref)
        part[...] = acc_ref[...].astype(bf16)
        backward_part(blocks, ins[-1], shift, fac_f, fac_g, acc_ref)
        gpart[...] = acc_ref[...].astype(bf16)

    def backward_body(blocks, shift, ins, outs, scratch):
        now, part = outs
        now[...] = total(ins[:3])
        backward_part(blocks, now, shift, ins[3], ins[4], scratch[0])
        part[...] = scratch[0][...].astype(bf16)

    def final_body(blocks, shift, ins, outs, scratch):
        acc_ref, now = scratch
        now[...] = total(ins[:3])
        backward_part(blocks, now, shift, ins[3], ins[4], acc_ref)
        even = lax.axis_index("chan") % 2 == 0
        for i in range(tm_count):
            cols = pl.ds(i * kb, kb)
            base = now[:, cols].astype(f32)
            value = acc_ref[:, cols] + jnp.where(even, base, jnp.zeros_like(base))
            out = sum(ins[n][:, cols].astype(f32) for n in (6, 7)) + ins[5][:, cols].astype(f32)
            if square:
                out = jnp.where(even, out[:, : kb // 2], out[:, kb // 2 :])
            for s in range(tm_count):
                part = slice(s * span, (s + 1) * span)
                outs[0][place(s, i), :, :kb] = value[part].astype(bf16)
                outs[0][place(s, i), :, kb:] = out[part].astype(bf16)

    factors, helds = [], []
    sig, grad, part, fac_f, fac_g, held = layer_call(
        0, first_body, [got], None, [act, act, act, fac, fac], acc, 1, "layer_first"
    )
    weights.own_halves([part])
    first_part = part
    for layer in range(1, layers - 1):
        arrived = swap(part)
        if layer == 1:
            middle = [p.array for p in weights.others[1]]
            arrived = lax.optimization_barrier((arrived, *middle))[0]
            pieces_of.append(weights.finish([first_part, *middle], [part]))
        factors.append((fac_f, fac_g))
        helds.append(held)
        sig, part, fac_f, fac_g, held = layer_call(
            layer, forward_body, [sig, part, arrived], None, [act, act, fac, fac], acc, 1, "layer_forward"
        )
    factors.append((fac_f, fac_g))
    helds.append(held)
    facs = [pltpu.VMEM((panels, m, nb), f32)] * 2
    sig, part, gpart, _ = layer_call(
        layers - 1,
        last_body,
        [sig, part, swap(part), grad],
        None,
        [act, act, act],
        facs + acc,
        2,
        "layer_last",
    )
    parts = [grad, gpart, swap(gpart)]
    output = [sig, part, swap(part)]
    for layer in reversed(range(1, layers - 1)):
        now, gpart = layer_call(
            layer,
            backward_body,
            [*parts, *factors[layer]],
            helds[layer],
            [act, act],
            acc,
            1,
            "layer_backward",
        )
        parts = [now, gpart, swap(gpart)]

    extra = kb // 2 if square else kb
    leaving = jax.ShapeDtypeStruct((tm_count * tm_count, span, kb + extra), bf16)
    back = layer_call(
        0,
        final_body,
        [*parts, *factors[0], *output],
        helds[0],
        [leaving],
        [*acc, pltpu.VMEM((m, width), bf16)],
        1,
        "layer_final",
    )[0]
    if not square:

        def regrouped(values):
            values = values.reshape(tm_count, tm_count, span, kb).transpose(0, 2, 1, 3)
            values = flipped(values.reshape(tm_count, span, width), tm_index, tm_count, kb)
            values = values.reshape(tm_count, span, chan_count, nb).transpose(0, 2, 1, 3)
            return values.reshape(peers, span, nb)

        out = regrouped(back[..., kb:])
        out = jnp.where(lax.axis_index("chan") % 2 == 0, out[..., : nb // 2], out[..., nb // 2 :])
        back = jnp.concatenate([regrouped(back[..., :kb]), out], axis=-1)
    back = lax.all_to_all(back, BOTH, split_axis=0, concat_axis=0, tiled=True)
    back = back.reshape(peers // 2, 2, span, nb + nb // 2)
    grads = back[..., :nb].astype(f32)
    input_grad = (grads[:, 0] + grads[:, 1]).astype(bf16).reshape(padded, nb)[:rows]
    output = jnp.concatenate([back[:, 0, :, nb:], back[:, 1, :, nb:]], axis=-1)
    return output.reshape(padded, nb)[:rows], input_grad


def solution(mesh):
    return jax.shard_map(
        local,
        mesh=mesh,
        in_specs=(
            P(("groups", "tm"), "chan"),
            P(("groups", "tm"), "chan"),
            P(None, None, "tm", "chan"),
            P(None, None, "tm", "chan"),
            P(None, "chan", "tm"),
        ),
        out_specs=(P(("groups", "tm"), "chan"), P(("groups", "tm"), "chan")),
        check_vma=False,
    )
```
